32 devices in a mesh: trial: 2 (over x), dp: 4 (over z), tensor: 4 (over y, core).
Axes of the slice: x: 2, y: 2, z: 4, core: 2. Of those that a mesh axis runs over, the one named last changes fastest.
Arguments:
- residual_rows: bfloat16 [1024, 8192], P(('trial', 'dp', 'tensor'))
- input_norm_weight: float32 [8192], replicated, may hold values from 0.25 to 1.75
- trial_row_index: int32 [2, 512], P(None, 'dp'), may hold values from 0 to 31, as said below
- keyvalue_weight: bfloat16 [8192, 2048], P('tensor'), may hold values from -0.0625 to 0.0625
- adapter_down_weight: bfloat16 [2, 8192, 128], P('trial', 'tensor'), may hold values from -0.0625 to 0.0625
- adapter_up_weight: bfloat16 [2, 64, 2048], P('trial'), may hold values from -0.75 to 0.75
- keyvalue_gradient: bfloat16 [2, 512, 2048], P('trial', ('dp', 'tensor')), may hold values from -6 to 6
Outputs:
- keyvalue_output: float32 [2, 512, 2048], P('trial', ('dp', 'tensor'))
- grad_a: float32 [2, 128, 8192], P('trial', 'dp', 'tensor')
- grad_b: float32 [2, 64, 2048], P('trial', None, ('dp', 'tensor'))
The draws below stay inside these ranges and needn't reach their ends.
Inputs may be any that keep to these rules, and one draw needn't show every extreme that they name: `trial_row_index`: within each trial, each index of dp and each block of 16 consecutive tokens taken from one source device, the rows named are distinct.
All inputs are finite; a program needn't handle non-finite values.
Results may differ from the reference program's by a relative error of at most 0.0041.
Values may be sent and summed in bfloat16 or wider, within the bound.
No kernel may reach another device: no remote copies, remote signals or barrier semaphores. Data moves between devices by JAX's collectives and lax.ppermute only.
A program may use at most 64 MiB of HBM per device.

```python
import math
import jax
import jax.numpy as jnp
from jax import lax

MODEL_WIDTH = 8192
KEYVALUE_WIDTH = 1024
ADAPTER_RANK = 64
SEL = 16
TRIAL_COUNT = 2
POOL_DEV = 32
POOL = 1024
TOK_DEV = 128
TOKENS = 512
N_TRIAL = 2
N_DP = 4
N_TENSOR = 4


def draw_residual_rows(key, part):
    key_vals, key_rows, key_cols = jax.random.split(key, 3)
    row_scale = jnp.exp(jax.random.uniform(key_rows, (POOL, 1), jnp.float32, 0.0, math.log(10.0)))
    col_scale = jnp.exp(jax.random.uniform(key_cols, (1, MODEL_WIDTH), jnp.float32, 0.0, math.log(10.0)))
    values = jax.random.normal(key_vals, (POOL, MODEL_WIDTH), jnp.float32)
    return (values * row_scale * col_scale).astype(jnp.bfloat16)


def draw_trial_row_index(key, part):
    groups = N_DP * N_TRIAL * N_TENSOR
    scores = jax.random.randint(key, (TRIAL_COUNT, groups, POOL_DEV), 0, 1048576, jnp.int32)
    scores = scores * POOL_DEV + jnp.arange(POOL_DEV, dtype=jnp.int32)[None, None, :]
    order = jnp.argsort(scores, axis=2).astype(jnp.int32)
    return order[:, :, :SEL].reshape(TRIAL_COUNT, TOKENS)


def raised(result, key, source, target, shards_of, factor):
    owner, partner = [(jnp.arange(result.shape[axis_at]) // (result.shape[axis_at] // shards_of)).reshape([-1 if axis == axis_at else 1 for axis in range(result.ndim)]) for axis_at in (source, target)]
    chosen = jax.random.permutation(key, shards_of)[partner]
    strong = (owner == chosen) | (owner == (partner + shards_of // 2) % shards_of)
    return jnp.where(strong, factor * result, result)


def levels(own_key, extent, cuts, least, top_value):
    loudness, own = 1.0, jax.random.fold_in(own_key, 6)
    for position, blocks in cuts:
        heights = jnp.exp(jax.random.uniform(jax.random.fold_in(own, position), (blocks,), jnp.float32, least / len(cuts), top_value / len(cuts)))
        loudness = loudness * jnp.repeat(heights, extent[position] // blocks).reshape([-1 if axis == position else 1 for axis in range(len(extent))])
    return loudness


def centred(key, dims, width, most, pieces=(), kind=jnp.bfloat16):
    entries = jax.random.normal(key, dims, jnp.float32) * width
    if len(pieces) > 0:
        entries = levels(key, dims, pieces, -0.22, 0.18) * entries
    return jnp.clip(entries, min=-most, max=most).astype(kind)


def heavy_noise(own_key, extent, deviation, bound, shards, heavy, kind=jnp.bfloat16):
    result = deviation * jax.random.normal(own_key, extent, jnp.float32)
    if shards:
        result = result * levels(own_key, extent, shards, -0.22, 0.18)
    return jnp.clip(raised(result, jax.random.fold_in(own_key, 3), *heavy), -bound, bound).astype(kind)


def setup_inputs(seed: int = 0) -> dict:
    splits = jax.random.split(jax.random.key(seed), 8)
    residual_rows = draw_residual_rows(jax.random.fold_in(splits[7], 71), 0)
    input_norm_weight = jnp.clip(1.0 + 0.15 * jax.random.normal(splits[1], (MODEL_WIDTH,), jnp.float32), 0.25, 1.75)
    trial_row_index = draw_trial_row_index(jax.random.fold_in(splits[7], 71), 0)
    keyvalue_weight = centred(splits[3], (MODEL_WIDTH, 2 * KEYVALUE_WIDTH), MODEL_WIDTH ** -0.5, 0.0625, ((0, 4),))
    adapter_down_weight = centred(splits[4], (TRIAL_COUNT, MODEL_WIDTH, 2 * ADAPTER_RANK), MODEL_WIDTH ** -0.5, 0.0625, ((0, 2), (1, 4)))
    adapter_up_weight = centred(splits[5], (TRIAL_COUNT, ADAPTER_RANK, 2 * KEYVALUE_WIDTH), ADAPTER_RANK ** -0.5, 0.75, ((0, 2),))
    keyvalue_gradient = heavy_noise(splits[6], (TRIAL_COUNT, TOKENS, 2 * KEYVALUE_WIDTH), 1.0, 6.0, ((0, 2), (1, 16)), (1, 2, 16, 2.0))
    return dict(residual_rows=residual_rows, input_norm_weight=input_norm_weight, trial_row_index=trial_row_index, keyvalue_weight=keyvalue_weight, adapter_down_weight=adapter_down_weight, adapter_up_weight=adapter_up_weight, keyvalue_gradient=keyvalue_gradient)


adapter_scale = 2.0
norm_eps = 1e-05

def reference(residual_rows, input_norm_weight, trial_row_index, keyvalue_weight, adapter_down_weight, adapter_up_weight, keyvalue_gradient):
    normed_input = MODEL_WIDTH // N_TENSOR
    tok = jnp.arange(TOKENS, dtype=jnp.int32)
    dp_index = tok // TOK_DEV
    source = tok % TOK_DEV // SEL
    source_trial = source // N_TENSOR
    source_tensor = source % N_TENSOR
    keyvalue_list = []
    grad_a_list = []
    up_gradient_list = []
    for trial_index in range(TRIAL_COUNT):
        index = ((source_trial * N_DP + dp_index) * N_TENSOR + source_tensor) * POOL_DEV + trial_row_index[trial_index]
        raw = residual_rows[index.astype(jnp.int32)].astype(jnp.float32)
        msq = lax.optimization_barrier(jnp.mean(raw * raw, axis=1, keepdims=True))
        x = (raw * lax.rsqrt(msq + norm_eps) * input_norm_weight[None, :]).astype(jnp.bfloat16)
        frozen_output = jnp.zeros((TOKENS, 2 * KEYVALUE_WIDTH), jnp.float32)
        down_product = jnp.zeros((TOKENS, 2 * ADAPTER_RANK), jnp.float32)
        for trial_position in range(N_TENSOR):
            row_portion = x[:, trial_position * normed_input:(trial_position + 1) * normed_input]
            part = jnp.dot(row_portion, keyvalue_weight[trial_position * normed_input:(trial_position + 1) * normed_input], preferred_element_type=jnp.float32)
            rank_portion = jnp.dot(row_portion, adapter_down_weight[trial_index][trial_position * normed_input:(trial_position + 1) * normed_input], preferred_element_type=jnp.float32)
            frozen_output = frozen_output + part
            down_product = down_product + rank_portion
        up_weight_full = adapter_up_weight[trial_index].astype(jnp.float32)
        precision_option = lax.Precision.HIGHEST
        adapter_key = jnp.dot(down_product[:, :ADAPTER_RANK], up_weight_full[:, :KEYVALUE_WIDTH], precision=precision_option)
        adapter_value = jnp.dot(down_product[:, ADAPTER_RANK:], up_weight_full[:, KEYVALUE_WIDTH:], precision=precision_option)
        keyvalue_list.append(frozen_output + adapter_scale * jnp.concatenate([adapter_key, adapter_value], axis=1))
        grad_in = keyvalue_gradient[trial_index].astype(jnp.float32)
        key_gradient_part = jnp.dot(grad_in[:, :KEYVALUE_WIDTH], up_weight_full[:, :KEYVALUE_WIDTH].T, precision=precision_option)
        value_gradient_part = jnp.dot(grad_in[:, KEYVALUE_WIDTH:], up_weight_full[:, KEYVALUE_WIDTH:].T, precision=precision_option)
        down_product_gradient = (adapter_scale * jnp.concatenate([key_gradient_part, value_gradient_part], axis=1)).astype(jnp.bfloat16)
        grad_a_list.append(lax.dot_general(down_product_gradient, x, (((0,), (0,)), ((), ())), preferred_element_type=jnp.float32))
        key_up_gradient = jnp.dot(down_product[:, :ADAPTER_RANK].T, grad_in[:, :KEYVALUE_WIDTH], precision=precision_option)
        value_up_gradient = jnp.dot(down_product[:, ADAPTER_RANK:].T, grad_in[:, KEYVALUE_WIDTH:], precision=precision_option)
        up_gradient_list.append(adapter_scale * jnp.concatenate([key_up_gradient, value_up_gradient], axis=1))
    return (jnp.stack(keyvalue_list), jnp.stack(grad_a_list), jnp.stack(up_gradient_list))
```

```python
import functools

import jax
import jax.numpy as jnp
from jax import lax
from jax.experimental import pallas as pl
from jax.experimental.pallas import tpu as pltpu
from jax.sharding import PartitionSpec as P

adapter_scale = 2.0
norm_eps = 1e-05
lanes = 128
f32 = jnp.float32
bf16 = jnp.bfloat16


def whole_vmem(count):
    return [pl.BlockSpec(memory_space=pltpu.VMEM)] * count


def params(mib):
    return pltpu.CompilerParams(vmem_limit_bytes=mib * 1024 * 1024)


def two_terms(value):
    high = value.astype(bf16)
    return high, (value - high.astype(f32)).astype(bf16)


def dot_rows(left, right):
    return lax.dot_general(left, right, (((0,), (0,)), ((), ())), preferred_element_type=f32)


def dot_last(left, right):
    return lax.dot_general(left, right, (((1,), (1,)), ((), ())), preferred_element_type=f32)


def pick_kernel(trials, ys, select, width, index_ref, rows_ref, gain_ref, grad_ref, up_ref, *rest):
    outs, chosen = rest[:-1], rest[-1]
    trial, tensor = lax.axis_index("trial"), lax.axis_index("tensor")
    tensors = 2 * ys
    y = tensor // 2
    pool, features = rows_ref.shape
    start = (trial * tensors + tensor) * select
    column = lax.broadcasted_iota(jnp.int32, (select, pool), 1)
    row = lax.broadcasted_iota(jnp.int32, (select, pool), 0)
    hots = []
    for a in range(trials):
        picked = jnp.zeros((select, pool), jnp.int32)
        for i in range(select):
            picked = jnp.where(row == i, index_ref[trial ^ a, start + i], picked)
        hots.append(jnp.where(column == picked, 1.0, 0.0).astype(bf16))
    hot = jnp.concatenate(hots, axis=0)
    square = jnp.zeros((trials * select, 1), f32)
    chunk = 1024
    for f in range(0, features, chunk):
        part = jnp.dot(hot, rows_ref[:, f : f + chunk], preferred_element_type=f32)
        chosen[:, f : f + chunk] = part
        square += jnp.sum(part * part, axis=1, keepdims=True)
    scale = lax.rsqrt(square / features + norm_eps)
    half = grad_ref.shape[2] // 2
    rank = up_ref.shape[1]
    keys = adapter_scale * dot_last(grad_ref[0, :, :half], up_ref[0, :, :half])
    values = adapter_scale * dot_last(grad_ref[0, :, half:], up_ref[0, :, half:])
    for a in range(trials):
        for b in range(ys):
            out = outs[a * ys + b]
            for core in range(2):
                for f in range(0, width, chunk):
                    at = pl.multiple_of((y ^ b) * (2 * width) + core * width + f, chunk)
                    part = chosen[a * select : (a + 1) * select, pl.ds(at, chunk)]
                    part = part * scale[a * select : (a + 1) * select] * gain_ref[:, pl.ds(at, chunk)]
                    out[core, :, f : f + chunk] = part.astype(bf16)
                if a == 0:
                    for j in range(trials // 2):
                        base = (2 * j + core) * select
                        lane = width + j * 2 * rank
                        out[core, :, lane : lane + rank] = keys[base : base + select].astype(bf16)
                        out[core, :, lane + rank : lane + 2 * rank] = values[base : base + select].astype(bf16)


def term_kernel(trials, ys, dps, select, width, *refs):
    count = trials * ys
    mine, other, down_ref = refs[:count], refs[count : 2 * count], refs[2 * count]
    rows_ref, rank_ref = refs[2 * count + 1], refs[2 * count + 2]
    terms, gradient = refs[2 * count + 3 : -1], refs[-1]
    trial, dp, tensor = lax.axis_index("trial"), lax.axis_index("dp"), lax.axis_index("tensor")
    tensors = 2 * ys
    y, core = tensor // 2, tensor % 2
    ranks = gradient.shape[1]
    local = trials * select
    for a in range(trials):
        for b in range(ys):
            for refs_at, from_core in ((mine, core), (other, 1 - core)):
                ref = refs_at[a * ys + b]
                member = 2 * (y ^ b) + from_core
                at = pl.multiple_of(((trial ^ a) * tensors + member) * select, select)
                rows_ref[pl.ds(at, select), :] = ref[core, :, :width]
                if a == 0:
                    for j in range(trials // 2):
                        for i in range(2):
                            to = pl.multiple_of(member * local + (2 * j + i) * select, select)
                            gradient[pl.ds(to, select), :] = ref[i, :, width + j * ranks : width + (j + 1) * ranks]
    rank_ref[...] = jnp.dot(rows_ref[...], down_ref[0], preferred_element_type=f32)
    block = ranks // dps
    turned = gradient[...].astype(f32).T.astype(bf16)
    chunk = 512
    for f in range(0, width, chunk):
        product = jnp.dot(turned, rows_ref[:, f : f + chunk], preferred_element_type=f32)
        terms[dps][:, f : f + chunk] = product
    full = terms[dps]
    for m in range(dps):
        at = pl.multiple_of((dp ^ m) * block, block)
        terms[m][...] = full[pl.ds(at, block), :].astype(terms[m].dtype)


def base_kernel(tensors, rows_ref, weight_ref, *refs):
    outs, total = refs[:-1], refs[-1]
    tensor = lax.axis_index("tensor")
    local = outs[0].shape[0]
    total[...] = jnp.dot(rows_ref[...], weight_ref[...], preferred_element_type=f32)
    for m in range(tensors):
        at = pl.multiple_of((tensor ^ m) * local, local)
        outs[m][...] = total[pl.ds(at, local), :].astype(outs[m].dtype)


def up_kernel(ys, dps, block, *refs):
    tensors = 2 * ys
    rank_refs, grads = refs[:ys], refs[ys : ys + tensors]
    outs, gradient, product = refs[ys + tensors : -2], refs[-2], refs[-1]
    dp, tensor = lax.axis_index("dp"), lax.axis_index("tensor")
    local, width = grads[0].shape[1], grads[0].shape[2]
    ranks = rank_refs[0].shape[1]
    ranks_sum = rank_refs[0][...]
    for ref in rank_refs[1:]:
        ranks_sum = ranks_sum + ref[...]
    high, low = two_terms(adapter_scale * ranks_sum.T)
    group = max(block, lanes)
    for m in range(tensors):
        at = pl.multiple_of((tensor ^ m) * local, local)
        for q in range(dps):
            place = pl.multiple_of((q * tensors + tensor) * block // group * group, group)
            gradient[pl.ds(at, local), q * group : (q + 1) * group] = grads[m][0, :, pl.ds(place, group)]
    values = gradient[...]
    product[...] = jnp.dot(high, values, preferred_element_type=f32) + jnp.dot(
        low, values, preferred_element_type=f32
    )
    for m in range(dps):
        for q in range(dps):

            @pl.when((dp ^ m) == q)
            def _():
                column = (q * tensors + tensor) * block
                upper = column // (width // 2)
                at = pl.multiple_of(upper * (ranks // 2), ranks // 2)
                part = product[pl.ds(at, ranks // 2), q * group : (q + 1) * group]
                if group > block:
                    inner = column % group
                    result = part[:, :block]
                    for i in range(1, group // block):
                        result = jnp.where(inner == i * block, part[:, i * block : (i + 1) * block], result)
                    part = result
                outs[m][...] = part.astype(outs[m].dtype)


def output_kernel(ys, *refs):
    tensors = 2 * ys
    rank_refs, terms, up_ref, out_ref = refs[:ys], refs[ys : ys + tensors], refs[-2], refs[-1]
    tensor = lax.axis_index("tensor")
    local, width = terms[0].shape
    half = width // 2
    rank = up_ref.shape[1]
    at = pl.multiple_of(tensor * local, local)
    ranks = rank_refs[0][pl.ds(at, local), :]
    for ref in rank_refs[1:]:
        ranks = ranks + ref[pl.ds(at, local), :]
    high, low = two_terms(adapter_scale * ranks)
    chunk = 512
    for f in range(0, width, chunk):
        side = rank * (f // half)
        up = up_ref[0, :, f : f + chunk]
        result = terms[0][:, f : f + chunk]
        for ref in terms[1:]:
            result = result + ref[:, f : f + chunk].astype(f32)
        result = result + jnp.dot(high[:, side : side + rank], up, preferred_element_type=f32)
        result = result + jnp.dot(low[:, side : side + rank], up, preferred_element_type=f32)
        out_ref[0, :, f : f + chunk] = result


def sum_kernel(count, *refs):
    for group in range(2):
        terms = refs[group * count : (group + 1) * count]
        out = refs[2 * count + group]
        result = terms[0][...]
        for ref in terms[1:]:
            result = result + ref[...].astype(f32)
        out[0] = result


def shards(
    residual_rows,
    input_norm_weight,
    trial_row_index,
    keyvalue_weight,
    adapter_down_weight,
    adapter_up_weight,
    keyvalue_gradient,
):
    trials, dps, tensors = lax.axis_size("trial"), lax.axis_size("dp"), lax.axis_size("tensor")
    ys = tensors // 2
    pool, features = residual_rows.shape
    tokens = trial_row_index.shape[1]
    select = tokens // (trials * tensors)
    local = tokens // tensors
    width, kv_width = keyvalue_weight.shape
    ranks = adapter_down_weight.shape[2]
    shape = jax.ShapeDtypeStruct

    def to_core(value):
        return lax.ppermute(value, "tensor", [(i, i ^ 1) for i in range(tensors)])

    def over(axis, size, mask, value):
        return lax.ppermute(value, axis, [(i, i ^ mask) for i in range(size)])

    extra = trials // 2 * ranks
    payload_shapes = [
        shape((2, select, width + (extra if a == 0 else 0)), bf16) for a in range(trials) for b in range(ys)
    ]
    payloads = pl.pallas_call(
        functools.partial(pick_kernel, trials, ys, select, width),
        out_shape=payload_shapes,
        in_specs=[pl.BlockSpec(memory_space=pltpu.SMEM)] + whole_vmem(4),
        out_specs=whole_vmem(len(payload_shapes)),
        scratch_shapes=[pltpu.VMEM((trials * select, features), f32)],
        compiler_params=params(32),
        name="pick",
    )(trial_row_index, residual_rows, input_norm_weight[None, :], keyvalue_gradient, adapter_up_weight)
    mine = [payloads[0]]
    for mask in range(1, trials * ys):
        a, b = mask // ys, mask % ys
        mine.append(over(("trial", "tensor"), trials * tensors, a * tensors + 2 * b, payloads[mask]))
    other = [to_core(value) for value in mine]

    block = ranks // dps
    rows, rank_term, *terms = pl.pallas_call(
        functools.partial(term_kernel, trials, ys, dps, select, width),
        out_shape=[shape((tokens, width), bf16), shape((tokens, ranks), f32), shape((block, width), f32)]
        + [shape((block, width), bf16)] * (dps - 1),
        in_specs=whole_vmem(2 * trials * ys + 1),
        out_specs=whole_vmem(2 + dps),
        scratch_shapes=[pltpu.VMEM((ranks, width), f32), pltpu.VMEM((tokens, ranks), bf16)],
        compiler_params=params(32),
        name="terms",
    )(*mine, *other, adapter_down_weight)
    down_terms = [terms[0]] + [over("dp", dps, m, terms[m]) for m in range(1, dps)]

    rank_pair = rank_term + to_core(rank_term)
    rank_sums = [rank_pair] + [over("tensor", tensors, 2 * b, rank_pair) for b in range(1, ys)]

    chunk = 512
    base_terms = pl.pallas_call(
        functools.partial(base_kernel, tensors),
        grid=(kv_width // chunk,),
        out_shape=[shape((local, kv_width), f32)] + [shape((local, kv_width), bf16)] * (tensors - 1),
        in_specs=[
            pl.BlockSpec((tokens, width), lambda n: (0, 0)),
            pl.BlockSpec((width, chunk), lambda n: (0, n)),
        ],
        out_specs=[pl.BlockSpec((local, chunk), lambda n: (0, n))] * tensors,
        scratch_shapes=[pltpu.VMEM((tokens, chunk), f32)],
        compiler_params=params(32),
        name="base",
    )(rows, keyvalue_weight)
    base_sums = [base_terms[0]] + [over("tensor", tensors, m, base_terms[m]) for m in range(1, tensors)]

    grads = [keyvalue_gradient] + [None] * (tensors - 1)
    for b in range(ys):
        if b:
            grads[2 * b] = over("tensor", tensors, 2 * b, keyvalue_gradient)
        grads[2 * b + 1] = to_core(grads[2 * b])
    column_block = kv_width // (dps * tensors)
    group = max(column_block, lanes)
    up_terms = pl.pallas_call(
        functools.partial(up_kernel, ys, dps, column_block),
        out_shape=[shape((ranks // 2, column_block), f32)] + [shape((ranks // 2, column_block), bf16)] * (dps - 1),
        in_specs=whole_vmem(ys + tensors),
        out_specs=whole_vmem(dps),
        scratch_shapes=[pltpu.VMEM((tokens, dps * group), bf16), pltpu.VMEM((ranks, dps * group), f32)],
        compiler_params=params(32),
        name="up_terms",
    )(*rank_sums, *grads)
    up_terms = [up_terms[0]] + [over("dp", dps, m, up_terms[m]) for m in range(1, dps)]

    output = pl.pallas_call(
        functools.partial(output_kernel, ys),
        out_shape=shape((1, local, kv_width), f32),
        in_specs=whole_vmem(ys + tensors + 1),
        out_specs=pl.BlockSpec(memory_space=pltpu.VMEM),
        compiler_params=params(32),
        name="output",
    )(*rank_sums, *base_sums, adapter_up_weight)
    grad_a, grad_b = pl.pallas_call(
        functools.partial(sum_kernel, dps),
        out_shape=[shape((1, block, width), f32), shape((1, ranks // 2, column_block), f32)],
        in_specs=whole_vmem(2 * dps),
        out_specs=whole_vmem(2),
        compiler_params=params(32),
        name="sums",
    )(*down_terms, *up_terms)
    return output, grad_a, grad_b


def solution(mesh):
    return jax.shard_map(
        shards,
        mesh=mesh,
        in_specs=(
            P(("trial", "dp", "tensor"), None),
            P(),
            P(None, "dp"),
            P("tensor", None),
            P("trial", "tensor", None),
            P("trial", None, None),
            P("trial", ("dp", "tensor"), None),
        ),
        out_specs=(
            P("trial", ("dp", "tensor"), None),
            P("trial", "dp", "tensor"),
            P("trial", None, ("dp", "tensor")),
        ),
        check_vma=False,
    )
```

```python
import functools

import jax
import jax.numpy as jnp
from jax import lax
from jax.experimental import pallas as pl
from jax.experimental.pallas import tpu as pltpu
from jax.sharding import PartitionSpec as P

adapter_scale = 2.0
norm_eps = 1e-05
lanes = 128
f32 = jnp.float32
bf16 = jnp.bfloat16


def whole_vmem(count):
    return [pl.BlockSpec(memory_space=pltpu.VMEM)] * count


def params(mib):
    return pltpu.CompilerParams(vmem_limit_bytes=mib * 1024 * 1024)


def in_hbm(count):
    return [pl.BlockSpec(memory_space=pltpu.HBM)] * count


def cost(flops, moved):
    return pl.CostEstimate(flops=flops, bytes_accessed=moved, transcendentals=0)


def two_terms(value):
    high = value.astype(bf16)
    return high, (value - high.astype(f32)).astype(bf16)


def dot_rows(left, right):
    return lax.dot_general(left, right, (((0,), (0,)), ((), ())), preferred_element_type=f32)


def dot_last(left, right):
    return lax.dot_general(left, right, (((1,), (1,)), ((), ())), preferred_element_type=f32)


def pick_kernel(trials, ys, dps, select, width, column_block, index_hbm, rows_hbm, gain_hbm, grad_hbm, up_hbm, down_hbm, *rest):
    outs, rest = rest[: trials * ys], rest[trials * ys :]
    downs = rest[:2]
    index_ref, rows_ref, gain_ref, grad_ref, up_ref, chosen, sems = rest[2:]
    copies = [
        pltpu.make_async_copy(source, target, sems.at[i])
        for i, (source, target) in enumerate(
            (
                (index_hbm, index_ref),
                (rows_hbm, rows_ref),
                (gain_hbm, gain_ref),
                (grad_hbm, grad_ref),
                (up_hbm, up_ref),
                (down_hbm.at[:, : width // 2], downs[0]),
                (down_hbm.at[:, width // 2 :], downs[1]),
            )
        )
    ]
    for copy in copies:
        copy.start()
    trial, tensor = lax.axis_index("trial"), lax.axis_index("tensor")
    tensors = 2 * ys
    y = tensor // 2
    pool, features = rows_ref.shape
    start = (trial * tensors + tensor) * select
    column = lax.broadcasted_iota(jnp.int32, (select, pool), 1)
    row = lax.broadcasted_iota(jnp.int32, (select, pool), 0)
    hots = []
    copies[0].wait()
    for a in range(trials):
        picked = jnp.zeros((select, pool), jnp.int32)
        for i in range(select):
            picked = jnp.where(row == i, index_ref[trial ^ a, start + i], picked)
        hots.append(jnp.where(column == picked, 1.0, 0.0).astype(bf16))
    hot = jnp.concatenate(hots, axis=0)
    square = jnp.zeros((trials * select, 1), f32)
    chunk = 1024
    copies[1].wait()
    for f in range(0, features, chunk):
        part = jnp.dot(hot, rows_ref[:, f : f + chunk], preferred_element_type=f32)
        chosen[:, f : f + chunk] = part
        square += jnp.sum(part * part, axis=1, keepdims=True)
    scale = lax.rsqrt(square / features + norm_eps)
    half = grad_ref.shape[2] // 2
    rank = up_ref.shape[1]
    for copy in copies[2:5]:
        copy.wait()
    keys = adapter_scale * dot_last(grad_ref[0, :, :half], up_ref[0, :, :half])
    values = adapter_scale * dot_last(grad_ref[0, :, half:], up_ref[0, :, half:])
    for a in range(trials):
        for b in range(ys):
            out = outs[a * ys + b]
            for core in range(2):
                for f in range(0, width, chunk):
                    at = pl.multiple_of((y ^ b) * (2 * width) + core * width + f, chunk)
                    part = chosen[a * select : (a + 1) * select, pl.ds(at, chunk)]
                    part = part * scale[a * select : (a + 1) * select] * gain_ref[:, pl.ds(at, chunk)]
                    out[core, :, f : f + chunk] = part.astype(bf16)
    group = max(column_block, lanes)
    for b in range(ys):
        for j in range(trials // 2):
            for core in range(2):
                token = (2 * j + core) * select
                at = slice(token, token + select)
                for i in range(2):
                    for q in range(dps):
                        member = 2 * (y ^ b) + i
                        place = pl.multiple_of((q * tensors + member) * column_block // group * group, group)
                        lane = width + ((2 * j + i) * dps + q) * group
                        outs[b][core, :, lane : lane + group] = grad_ref[0, at, pl.ds(place, group)]
                lane = width + trials * dps * group + j * 2 * rank
                outs[b][core, :, lane : lane + rank] = keys[at].astype(bf16)
                outs[b][core, :, lane + rank : lane + 2 * rank] = values[at].astype(bf16)
    copies[5].wait()
    copies[6].wait()


def term_kernel(trials, ys, dps, select, width, *refs):
    count = trials * ys
    far = dps // 2 - 1
    mine, other, refs = refs[:count], refs[count : 2 * count], refs[2 * count :]
    downs, refs = refs[:4], refs[4:]
    rows_ref, turned_ref, rank_ref = refs[:3]
    terms = refs[3 : 3 + far]
    pair, gradient, turned = refs[3 + far :]
    trial, dp, tensor = lax.axis_index("trial"), lax.axis_index("dp"), lax.axis_index("tensor")
    tensors = 2 * ys
    y, core = tensor // 2, tensor % 2
    ranks = gradient.shape[1]
    local = trials * select
    for a in range(trials):
        for b in range(ys):
            for refs_at, from_core in ((mine, core), (other, 1 - core)):
                ref = refs_at[a * ys + b]
                member = 2 * (y ^ b) + from_core
                at = pl.multiple_of(((trial ^ a) * tensors + member) * select, select)
                for i in range(2):
                    pair[i, pl.ds(at, select), :] = ref[i, :, :width]
                if a == 0:
                    for j in range(trials // 2):
                        lane = ref.shape[2] - (trials // 2 - j) * ranks
                        for i in range(2):
                            to = pl.multiple_of(member * local + (2 * j + i) * select, select)
                            gradient[pl.ds(to, select), :] = ref[i, :, lane : lane + ranks]
    block = ranks // dps
    turned[...] = gradient[...].astype(f32).T
    turned_ref[...] = turned[...].astype(bf16)
    for j in range(far):
        at = pl.multiple_of((dp ^ (2 * (j + 1) + core)) * block, block)
        part = turned[pl.ds(at, block), :].astype(bf16)
        for i in range(2):
            terms[j][i] = jnp.dot(part, pair[i], preferred_element_type=f32).astype(bf16)
    rows_ref[...] = pair[core]
    result = jnp.zeros(rank_ref.shape, f32)
    for n, ref in enumerate(downs):
        i = core if n < 2 else 1 - core
        at = slice(n % 2 * (width // 2), (n % 2 + 1) * (width // 2))
        result += jnp.dot(pair[i, :, at], ref[0], preferred_element_type=f32)
    rank_ref[...] = result


def base_kernel(ys, rows_ref, weight_ref, *refs):
    kept, sent, total = refs[:ys], refs[ys : 2 * ys], refs[-1]
    tensor = lax.axis_index("tensor")
    local, width = kept[0].shape
    chunk = 512
    for f in range(0, width, chunk):
        total[:, f : f + chunk] = jnp.dot(rows_ref[...], weight_ref[:, f : f + chunk], preferred_element_type=f32)
        for b in range(ys):
            for out, member in ((kept[b], tensor ^ (2 * b)), (sent[b], tensor ^ (2 * b + 1))):
                at = pl.multiple_of(member * local, local)
                out[:, f : f + chunk] = total[pl.ds(at, local), f : f + chunk].astype(out.dtype)


def pair_kernel(kept_ref, came_ref, out_ref):
    out_ref[...] = (kept_ref[...] + came_ref[...].astype(f32)).astype(bf16)


def up_kernel(trials, ys, dps, select, block, *refs):
    tensors = 2 * ys
    far = dps // 2 - 1
    rank_refs, mine, other = refs[:ys], refs[ys : 2 * ys], refs[2 * ys : 3 * ys]
    rows_ref, turned_ref = refs[3 * ys : 3 * ys + 2]
    down_own, up_own, near = refs[3 * ys + 2 : 3 * ys + 5]
    outs, gradient, product = refs[3 * ys + 5 : -2], refs[-2], refs[-1]
    dp, tensor = lax.axis_index("dp"), lax.axis_index("tensor")
    y, core = tensor // 2, tensor % 2
    local = trials * select
    half = dps * tensors * block // 2
    width = rows_ref.shape[1]
    ranks = rank_refs[0].shape[1]
    rank = ranks // 2
    down_block = ranks // dps
    group = max(block, lanes)
    ranks_sum = rank_refs[0][...]
    for ref in rank_refs[1:]:
        ranks_sum = ranks_sum + ref[...]
    high, low = two_terms(adapter_scale * ranks_sum.T)
    for i in range(2):
        for b in range(ys):
            for ref, from_core in ((mine[b], core), (other[b], 1 - core)):
                for j in range(trials // 2):
                    lane = width + (2 * j + i) * dps * group
                    for n in range(2):
                        token = (2 * (y ^ b) + from_core) * local + (2 * j + n) * select
                        at = pl.multiple_of(token, select)
                        gradient[i, pl.ds(at, select), :] = ref[n, :, lane : lane + dps * group]
    for i in range(2):
        values = gradient[i]
        product[i] = jnp.dot(high, values, preferred_element_type=f32) + jnp.dot(
            low, values, preferred_element_type=f32
        )

    def up_part(target, i):
        column = (target * tensors + 2 * y + i) * block
        upper = column // half
        at = pl.multiple_of(upper * rank, rank)
        part = product[i, pl.ds(at, rank), pl.ds(pl.multiple_of(target * group, group), group)]
        if group > block:
            inner = column % group
            result = part[:, :block]
            for n in range(1, group // block):
                result = jnp.where(inner == n * block, part[:, n * block : (n + 1) * block], result)
            part = result
        return part

    for j in range(far):
        for i in range(2):
            outs[j][i] = up_part(dp ^ (2 * (j + 1) + core), i).astype(bf16)
    for target, out in ((dp ^ 1, near), (dp, None)):
        at = pl.multiple_of(target * down_block, down_block)
        term = jnp.dot(turned_ref[pl.ds(at, down_block), :], rows_ref[...], preferred_element_type=f32)
        part = up_part(target, core)
        if out is None:
            down_own[...] = term
            up_own[...] = part
        else:
            out[:, :width] = term.astype(bf16)
            for n in range(rank // down_block):
                lane = width + n * block
                out[:, lane : lane + block] = part[n * down_block : (n + 1) * down_block].astype(bf16)


def output_kernel(ys, *refs):
    rank_refs, terms, up_ref, out_ref = refs[:ys], refs[ys:-2], refs[-2], refs[-1]
    tensor = lax.axis_index("tensor")
    local, width = terms[0].shape
    half = width // 2
    rank = up_ref.shape[1]
    at = pl.multiple_of(tensor * local, local)
    ranks = rank_refs[0][pl.ds(at, local), :]
    for ref in rank_refs[1:]:
        ranks = ranks + ref[pl.ds(at, local), :]
    high, low = two_terms(adapter_scale * ranks)
    chunk = 512
    for f in range(0, width, chunk):
        side = rank * (f // half)
        up = up_ref[0, :, f : f + chunk]
        result = terms[0][:, f : f + chunk]
        for ref in terms[1:]:
            result = result + ref[:, f : f + chunk].astype(f32)
        result = result + jnp.dot(high[:, side : side + rank], up, preferred_element_type=f32)
        result = result + jnp.dot(low[:, side : side + rank], up, preferred_element_type=f32)
        out_ref[0, :, f : f + chunk] = result


def split_kernel(pieces, term_ref, up_ref, _near, *outs):
    core = lax.axis_index("tensor") % 2
    down_block, width = term_ref.shape[1:]
    block = up_ref.shape[2]
    size = width // pieces
    for n in range(pieces):
        outs[n][:, :size] = term_ref[1 - core, :, n * size : (n + 1) * size]
    for n in range(up_ref.shape[1] // down_block):
        lane = size + n // pieces * block
        outs[n % pieces][:, lane : lane + block] = up_ref[1 - core, n * down_block : (n + 1) * down_block, :]


def sum_kernel(far, pieces, *refs):
    down_own, up_own, near = refs[:3]
    downs, refs = refs[3 : 3 + far], refs[3 + far :]
    ups, refs = refs[:far], refs[far:]
    others = refs[: far * pieces]
    down_out, up_out = refs[far * pieces :]
    core = lax.axis_index("tensor") % 2
    down_block, width = down_own.shape
    rank, block = up_own.shape
    size = width // pieces
    for n in range(pieces):
        at = slice(n * size, (n + 1) * size)
        result = down_own[:, at] + near[:, at].astype(f32)
        for j in range(far):
            result = result + downs[j][core, :, at].astype(f32)
            result = result + others[j * pieces + n][:, :size].astype(f32)
        down_out[0, :, at] = result
    for n in range(rank // down_block):
        at = slice(n * down_block, (n + 1) * down_block)
        result = up_own[at, :] + near[:, width + n * block : width + (n + 1) * block].astype(f32)
        lane = size + n // pieces * block
        for j in range(far):
            result = result + ups[j][core, at, :].astype(f32)
            result = result + others[j * pieces + n % pieces][:, lane : lane + block].astype(f32)
        up_out[0, at, :] = result


def shards(
    residual_rows,
    input_norm_weight,
    trial_row_index,
    keyvalue_weight,
    adapter_down_weight,
    adapter_up_weight,
    keyvalue_gradient,
):
    trials, dps, tensors = lax.axis_size("trial"), lax.axis_size("dp"), lax.axis_size("tensor")
    ys = tensors // 2
    pool, features = residual_rows.shape
    tokens = trial_row_index.shape[1]
    select = tokens // (trials * tensors)
    local = tokens // tensors
    width, kv_width = keyvalue_weight.shape
    ranks = adapter_down_weight.shape[2]
    shape = jax.ShapeDtypeStruct

    def to_core(value):
        return lax.ppermute(value, "tensor", [(i, i ^ 1) for i in range(tensors)])

    def over(axis, size, mask, value):
        return lax.ppermute(value, axis, [(i, i ^ mask) for i in range(size)])

    def far_dp(j, value):
        pairs = []
        for source in range(dps):
            for member in range(tensors):
                target = source ^ (2 * (j + 1) + member % 2)
                pairs.append((source * tensors + member, target * tensors + member))
        return lax.ppermute(value, ("dp", "tensor"), pairs)

    far = dps // 2 - 1
    block = ranks // dps
    column_block = kv_width // (dps * tensors)
    group = max(column_block, lanes)
    extra = trials * dps * group + trials // 2 * ranks
    payload_shapes = [
        shape((2, select, width + (extra if a == 0 else 0)), bf16) for a in range(trials) for b in range(ys)
    ]
    gain = input_norm_weight[None, :]
    pick_operands = (
        trial_row_index,
        residual_rows,
        gain,
        keyvalue_gradient,
        adapter_up_weight,
        adapter_down_weight,
    )
    picked = pl.pallas_call(
        functools.partial(pick_kernel, trials, ys, dps, select, width, column_block),
        out_shape=payload_shapes + [shape((1, width // 2, ranks), bf16)] * 2,
        in_specs=in_hbm(6),
        out_specs=whole_vmem(len(payload_shapes) + 2),
        scratch_shapes=[pltpu.SMEM(trial_row_index.shape, jnp.int32)]
        + [pltpu.VMEM(value.shape, value.dtype) for value in pick_operands[1:5]]
        + [pltpu.VMEM((trials * select, features), f32), pltpu.SemaphoreType.DMA((7,))],
        compiler_params=params(32),
        name="pick",
    )(*[pltpu.with_memory_space_constraint(value, pltpu.HBM) for value in pick_operands])
    payloads, downs = picked[:-2], picked[-2:]
    mine = [payloads[0]] + [None] * (trials * ys - 1)
    for mask in range(1, trials * ys):
        a, b = mask // ys, mask % ys
        mine[mask] = over(("trial", "tensor"), trials * tensors, a * tensors + 2 * b, payloads[mask])
    other = [to_core(value) for value in mine]
    downs = [*downs, *[to_core(value) for value in downs]]

    rows, turned, rank_term, *terms = pl.pallas_call(
        functools.partial(term_kernel, trials, ys, dps, select, width),
        out_shape=[shape((tokens, width), bf16), shape((ranks, tokens), bf16), shape((tokens, ranks), f32)]
        + [shape((2, block, width), bf16)] * far,
        in_specs=whole_vmem(2 * trials * ys + 4),
        out_specs=whole_vmem(3 + far),
        scratch_shapes=[
            pltpu.VMEM((2, tokens, width), bf16),
            pltpu.VMEM((tokens, ranks), bf16),
            pltpu.VMEM((ranks, tokens), f32),
        ],
        compiler_params=params(16),
        cost_estimate=cost(2 * 10**10, 2 * 10**7),
        name="terms",
    )(*mine, *other, *downs)
    down_far = [far_dp(j, terms[j]) for j in range(far)]
    rank_sums = [rank_term] + [over("tensor", tensors, 2 * b, rank_term) for b in range(1, ys)]

    base_terms = pl.pallas_call(
        functools.partial(base_kernel, ys),
        out_shape=[shape((local, kv_width), f32)] * ys + [shape((local, kv_width), bf16)] * ys,
        in_specs=whole_vmem(2),
        out_specs=whole_vmem(2 * ys),
        scratch_shapes=[pltpu.VMEM((tokens, kv_width), f32)],
        compiler_params=params(8),
        cost_estimate=cost(0, 0),
        name="base",
    )(rows, keyvalue_weight)
    kept = base_terms[:ys]
    came = [None] * ys
    for b in [*range(1, ys), 0]:
        came[b] = to_core(base_terms[ys + b])
    base_sums = [kept[0], came[0]]
    for b in range(1, ys):
        paired = pl.pallas_call(
            pair_kernel,
            out_shape=shape((local, kv_width), bf16),
            in_specs=whole_vmem(2),
            out_specs=pl.BlockSpec(memory_space=pltpu.VMEM),
            compiler_params=params(4),
            cost_estimate=cost(0, 0),
            name="pair",
        )(kept[b], came[b])
        base_sums.append(over("tensor", tensors, 2 * b, paired))

    down_own, up_own, near, *up_far = pl.pallas_call(
        functools.partial(up_kernel, trials, ys, dps, select, column_block),
        out_shape=[
            shape((block, width), f32),
            shape((ranks // 2, column_block), f32),
            shape((block, width + ranks // 2 // block * column_block), bf16),
        ]
        + [shape((2, ranks // 2, column_block), bf16)] * far,
        in_specs=whole_vmem(3 * ys + 2),
        out_specs=whole_vmem(3 + far),
        scratch_shapes=[pltpu.VMEM((2, tokens, dps * group), bf16), pltpu.VMEM((2, ranks, dps * group), f32)],
        compiler_params=params(8),
        cost_estimate=cost(0, 0),
        name="up_terms",
    )(*rank_sums, *mine[:ys], *other[:ys], rows, turned)
    near = over("dp", dps, 1, near)
    up_far = [far_dp(j, up_far[j]) for j in range(far)]
    output = pl.pallas_call(
        functools.partial(output_kernel, ys),
        out_shape=shape((1, local, kv_width), f32),
        in_specs=whole_vmem(2 * ys + 2),
        out_specs=pl.BlockSpec(memory_space=pltpu.VMEM),
        compiler_params=params(8),
        cost_estimate=cost(0, 0),
        name="output",
    )(*rank_sums, *base_sums, adapter_up_weight)
    pieces = 2
    up_lanes = ranks // 2 // block // pieces * column_block
    others = []
    for down_value, up_value in zip(down_far, up_far):
        parts = pl.pallas_call(
            functools.partial(split_kernel, pieces),
            out_shape=[shape((block, width // pieces + up_lanes), bf16)] * pieces,
            in_specs=whole_vmem(3),
            out_specs=whole_vmem(pieces),
            compiler_params=params(4),
            cost_estimate=cost(0, 0),
            name="split",
        )(down_value, up_value, near)
        others += [to_core(part) for part in parts]

    grad_a, grad_b = pl.pallas_call(
        functools.partial(sum_kernel, far, pieces),
        out_shape=[shape((1, block, width), f32), shape((1, ranks // 2, column_block), f32)],
        in_specs=whole_vmem(3 + (2 + pieces) * far),
        out_specs=whole_vmem(2),
        compiler_params=params(8),
        cost_estimate=cost(0, 0),
        name="sums",
    )(down_own, up_own, near, *down_far, *up_far, *others)
    return output, grad_a, grad_b


def solution(mesh):
    return jax.shard_map(
        shards,
        mesh=mesh,
        in_specs=(
            P(("trial", "dp", "tensor"), None),
            P(),
            P(None, "dp"),
            P("tensor", None),
            P("trial", "tensor", None),
            P("trial", None, None),
            P("trial", ("dp", "tensor"), None),
        ),
        out_specs=(
            P("trial", ("dp", "tensor"), None),
            P("trial", "dp", "tensor"),
            P("trial", None, ("dp", "tensor")),
        ),
        check_vma=False,
    )
```

```python
import functools

import jax
import jax.numpy as jnp
from jax import lax
from jax.experimental import pallas as pl
from jax.experimental.pallas import tpu as pltpu
from jax.sharding import PartitionSpec as P

adapter_scale = 2.0
norm_eps = 1e-05
lanes = 128
f32 = jnp.float32
bf16 = jnp.bfloat16


def whole_vmem(count):
    return [pl.BlockSpec(memory_space=pltpu.VMEM)] * count


def params(mib):
    return pltpu.CompilerParams(vmem_limit_bytes=mib * 1024 * 1024)


def in_hbm(count):
    return [pl.BlockSpec(memory_space=pltpu.HBM)] * count


def cost(flops, moved):
    return pl.CostEstimate(flops=flops, bytes_accessed=moved, transcendentals=0)


def two_terms(value):
    high = value.astype(bf16)
    return high, (value - high.astype(f32)).astype(bf16)


def dot_rows(left, right):
    return lax.dot_general(left, right, (((0,), (0,)), ((), ())), preferred_element_type=f32)


def dot_last(left, right):
    return lax.dot_general(left, right, (((1,), (1,)), ((), ())), preferred_element_type=f32)


def pick_kernel(trials, ys, dps, select, width, column_block, index_hbm, rows_hbm, gain_hbm, grad_hbm, up_hbm, down_hbm, *rest):
    outs, rest = rest[: trials * ys], rest[trials * ys :]
    downs = rest[:2]
    index_ref, rows_ref, gain_ref, grad_ref, up_ref, sems = rest[2:]
    copies = [
        pltpu.make_async_copy(source, target, sems.at[i])
        for i, (source, target) in enumerate(
            (
                (index_hbm, index_ref),
                (rows_hbm, rows_ref),
                (gain_hbm, gain_ref),
                (grad_hbm, grad_ref),
                (up_hbm, up_ref),
                (down_hbm.at[:, : width // 2], downs[0]),
                (down_hbm.at[:, width // 2 :], downs[1]),
            )
        )
    ]
    for copy in copies:
        copy.start()
    trial, tensor = lax.axis_index("trial"), lax.axis_index("tensor")
    tensors = 2 * ys
    y = tensor // 2
    pool, features = rows_ref.shape
    start = (trial * tensors + tensor) * select
    column = lax.broadcasted_iota(jnp.int32, (select, pool), 1)
    row = lax.broadcasted_iota(jnp.int32, (select, pool), 0)
    hots = []
    copies[0].wait()
    for a in range(trials):
        picked = jnp.zeros((select, pool), jnp.int32)
        for i in range(select):
            picked = jnp.where(row == i, index_ref[trial ^ a, start + i], picked)
        hots.append(jnp.where(column == picked, 1.0, 0.0).astype(bf16))
    hot = jnp.concatenate(hots, axis=0)
    square = jnp.zeros((pool, 1), f32)
    chunk = 1024
    copies[1].wait()
    for f in range(0, features, chunk):
        part = rows_ref[:, f : f + chunk].astype(f32)
        square += jnp.sum(part * part, axis=1, keepdims=True)
    scale = lax.rsqrt(square / features + norm_eps)
    half = grad_ref.shape[2] // 2
    rank = up_ref.shape[1]
    for copy in copies[2:5]:
        copy.wait()
    keys = adapter_scale * dot_last(grad_ref[0, :, :half], up_ref[0, :, :half])
    values = adapter_scale * dot_last(grad_ref[0, :, half:], up_ref[0, :, half:])
    for b in range(ys):
        for core in range(2):
            for f in range(0, width, chunk):
                at = pl.multiple_of((y ^ b) * (2 * width) + core * width + f, chunk)
                part = rows_ref[:, pl.ds(at, chunk)].astype(f32) * scale * gain_ref[:, pl.ds(at, chunk)]
                part = jnp.dot(hot, part.astype(bf16), preferred_element_type=f32).astype(bf16)
                for a in range(trials):
                    outs[a * ys + b][core, :, f : f + chunk] = part[a * select : (a + 1) * select]
    group = max(column_block, lanes)
    for b in range(ys):
        for j in range(trials // 2):
            for core in range(2):
                token = (2 * j + core) * select
                at = slice(token, token + select)
                for i in range(2):
                    for q in range(dps):
                        member = 2 * (y ^ b) + i
                        place = pl.multiple_of((q * tensors + member) * column_block // group * group, group)
                        lane = width + ((2 * j + i) * dps + q) * group
                        outs[b][core, :, lane : lane + group] = grad_ref[0, at, pl.ds(place, group)]
                lane = width + trials * dps * group + j * 2 * rank
                outs[b][core, :, lane : lane + rank] = keys[at].astype(bf16)
                outs[b][core, :, lane + rank : lane + 2 * rank] = values[at].astype(bf16)
    copies[5].wait()
    copies[6].wait()


def term_kernel(trials, ys, dps, select, width, *refs):
    count = trials * ys
    far = dps // 2 - 1
    mine, other, refs = refs[:count], refs[count : 2 * count], refs[2 * count :]
    pair, turned_ref = refs[:2]
    terms = refs[2 : 2 + far]
    gradient, turned = refs[2 + far :]
    trial, dp, tensor = lax.axis_index("trial"), lax.axis_index("dp"), lax.axis_index("tensor")
    tensors = 2 * ys
    y, core = tensor // 2, tensor % 2
    ranks = gradient.shape[1]
    local = trials * select
    for a in range(trials):
        for b in range(ys):
            for refs_at, from_core in ((mine, core), (other, 1 - core)):
                ref = refs_at[a * ys + b]
                member = 2 * (y ^ b) + from_core
                at = pl.multiple_of(((trial ^ a) * tensors + member) * select, select)
                for i in range(2):
                    pair[i, pl.ds(at, select), :] = ref[i, :, :width]
                if a == 0:
                    for j in range(trials // 2):
                        lane = ref.shape[2] - (trials // 2 - j) * ranks
                        for i in range(2):
                            to = pl.multiple_of(member * local + (2 * j + i) * select, select)
                            gradient[pl.ds(to, select), :] = ref[i, :, lane : lane + ranks]
    block = ranks // dps
    turned[...] = gradient[...].astype(f32).T
    turned_ref[...] = turned[...].astype(bf16)
    for j in range(far):
        at = pl.multiple_of((dp ^ (2 * (j + 1) + core)) * block, block)
        part = turned[pl.ds(at, block), :].astype(bf16)
        for i in range(2):
            first = terms[j].shape[2]
            terms[j][i] = jnp.dot(part, pair[i, :, :first], preferred_element_type=f32).astype(bf16)


def rank_kernel(pair, *refs):
    downs, rank_ref = refs[:4], refs[4]
    core = lax.axis_index("tensor") % 2
    result = jnp.zeros(rank_ref.shape, f32)
    for n, ref in enumerate(downs):
        i = core if n < 2 else 1 - core
        size = ref.shape[1]
        result += jnp.dot(pair[i, :, n % 2 * size : (n % 2 + 1) * size], ref[0], preferred_element_type=f32)
    rank_ref[...] = result


def base_kernel(ys, pair, weight_ref, *refs):
    kept, sent, total = refs[:ys], refs[ys : 2 * ys], refs[-1]
    tensor = lax.axis_index("tensor")
    local, width = kept[0].shape
    chunk = 512
    for f in range(0, width, chunk):
        total[:, f : f + chunk] = jnp.dot(pair[tensor % 2], weight_ref[:, f : f + chunk], preferred_element_type=f32)
        for b in range(ys):
            for out, member in ((kept[b], tensor ^ (2 * b)), (sent[b], tensor ^ (2 * b + 1))):
                at = pl.multiple_of(member * local, local)
                out[:, f : f + chunk] = total[pl.ds(at, local), f : f + chunk].astype(out.dtype)


def pair_kernel(kept_ref, came_ref, out_ref):
    out_ref[...] = (kept_ref[...] + came_ref[...].astype(f32)).astype(bf16)


def up_kernel(trials, ys, dps, select, block, *refs):
    tensors = 2 * ys
    far = dps // 2 - 1
    rank_refs, mine, other = refs[:ys], refs[ys : 2 * ys], refs[2 * ys : 3 * ys]
    pair, turned_ref = refs[3 * ys : 3 * ys + 2]
    down_own, up_own, near = refs[3 * ys + 2 : 3 * ys + 5]
    outs, gradient, product = refs[3 * ys + 5 : -2], refs[-2], refs[-1]
    dp, tensor = lax.axis_index("dp"), lax.axis_index("tensor")
    y, core = tensor // 2, tensor % 2
    local = trials * select
    half = dps * tensors * block // 2
    width = pair.shape[2]
    ranks = rank_refs[0].shape[1]
    rank = ranks // 2
    down_block = ranks // dps
    group = max(block, lanes)
    ranks_sum = rank_refs[0][...]
    for ref in rank_refs[1:]:
        ranks_sum = ranks_sum + ref[...]
    high, low = two_terms(adapter_scale * ranks_sum.T)
    for i in range(2):
        for b in range(ys):
            for ref, from_core in ((mine[b], core), (other[b], 1 - core)):
                for j in range(trials // 2):
                    lane = width + (2 * j + i) * dps * group
                    for n in range(2):
                        token = (2 * (y ^ b) + from_core) * local + (2 * j + n) * select
                        at = pl.multiple_of(token, select)
                        gradient[i, pl.ds(at, select), :] = ref[n, :, lane : lane + dps * group]
    for i in range(2):
        values = gradient[i]
        product[i] = jnp.dot(high, values, preferred_element_type=f32) + jnp.dot(
            low, values, preferred_element_type=f32
        )

    def up_part(target, i):
        column = (target * tensors + 2 * y + i) * block
        upper = column // half
        at = pl.multiple_of(upper * rank, rank)
        part = product[i, pl.ds(at, rank), pl.ds(pl.multiple_of(target * group, group), group)]
        if group > block:
            inner = column % group
            result = part[:, :block]
            for n in range(1, group // block):
                result = jnp.where(inner == n * block, part[:, n * block : (n + 1) * block], result)
            part = result
        return part

    for j in range(far):
        size = outs[j].shape[2] - rank // down_block * block
        at = pl.multiple_of((dp ^ (2 * (j + 1) + core)) * down_block, down_block)
        for i in range(2):
            term = jnp.dot(turned_ref[pl.ds(at, down_block), :], pair[i, :, width - size :], preferred_element_type=f32)
            outs[j][i, :, :size] = term.astype(bf16)
            part = up_part(dp ^ (2 * (j + 1) + core), i).astype(bf16)
            for n in range(rank // down_block):
                lane = size + n * block
                outs[j][i, :, lane : lane + block] = part[n * down_block : (n + 1) * down_block]
    for target, out in ((dp ^ 1, near), (dp, None)):
        at = pl.multiple_of(target * down_block, down_block)
        term = jnp.dot(turned_ref[pl.ds(at, down_block), :], pair[core], preferred_element_type=f32)
        part = up_part(target, core)
        if out is None:
            down_own[...] = term
            up_own[...] = part
        else:
            out[:, :width] = term.astype(bf16)
            for n in range(rank // down_block):
                lane = width + n * block
                out[:, lane : lane + block] = part[n * down_block : (n + 1) * down_block].astype(bf16)


def output_kernel(ys, *refs):
    rank_refs, terms, up_ref, out_ref = refs[:ys], refs[ys:-2], refs[-2], refs[-1]
    tensor = lax.axis_index("tensor")
    local, width = terms[0].shape
    half = width // 2
    rank = up_ref.shape[1]
    at = pl.multiple_of(tensor * local, local)
    ranks = rank_refs[0][pl.ds(at, local), :]
    for ref in rank_refs[1:]:
        ranks = ranks + ref[pl.ds(at, local), :]
    high, low = two_terms(adapter_scale * ranks)
    chunk = 512
    for f in range(0, width, chunk):
        side = rank * (f // half)
        up = up_ref[0, :, f : f + chunk]
        result = terms[0][:, f : f + chunk]
        for ref in terms[1:]:
            result = result + ref[:, f : f + chunk].astype(f32)
        result = result + jnp.dot(high[:, side : side + rank], up, preferred_element_type=f32)
        result = result + jnp.dot(low[:, side : side + rank], up, preferred_element_type=f32)
        out_ref[0, :, f : f + chunk] = result


def split_kernel(*refs):
    term_ref, out_ref = refs[0], refs[-1]
    size = term_ref.shape[2]
    out_ref[:, :size] = term_ref[1 - lax.axis_index("tensor") % 2]
    if out_ref.shape[1] > size:
        out_ref[:, size:] = jnp.zeros((out_ref.shape[0], out_ref.shape[1] - size), bf16)


def sum_kernel(far, *refs):
    down_own, up_own, near = refs[:3]
    firsts, seconds = refs[3 : 3 + far], refs[3 + far : 3 + 2 * far]
    others, (down_out, up_out) = refs[3 + 2 * far : -2], refs[-2:]
    core = lax.axis_index("tensor") % 2
    down_block, width = down_own.shape
    rank, block = up_own.shape
    first = firsts[0].shape[2]

    def total(result, lane, size):
        result = result + near[:, lane : lane + size].astype(f32)
        for j in range(far):
            if lane < first:
                result = result + firsts[j][core].astype(f32) + others[j][...].astype(f32)
            else:
                at = slice(lane - first, lane - first + size)
                result = result + seconds[j][core, :, at].astype(f32) + others[far + j][:, at].astype(f32)
        return result

    down_out[0, :, :first] = total(down_own[:, :first], 0, first)
    down_out[0, :, first:] = total(down_own[:, first:], first, width - first)
    for n in range(rank // down_block):
        at = slice(n * down_block, (n + 1) * down_block)
        up_out[0, at, :] = total(up_own[at, :], width + n * block, block)


def shards(
    residual_rows,
    input_norm_weight,
    trial_row_index,
    keyvalue_weight,
    adapter_down_weight,
    adapter_up_weight,
    keyvalue_gradient,
):
    trials, dps, tensors = lax.axis_size("trial"), lax.axis_size("dp"), lax.axis_size("tensor")
    ys = tensors // 2
    pool, features = residual_rows.shape
    tokens = trial_row_index.shape[1]
    select = tokens // (trials * tensors)
    local = tokens // tensors
    width, kv_width = keyvalue_weight.shape
    ranks = adapter_down_weight.shape[2]
    shape = jax.ShapeDtypeStruct

    def to_core(value):
        return lax.ppermute(value, "tensor", [(i, i ^ 1) for i in range(tensors)])

    def over(axis, size, mask, value):
        return lax.ppermute(value, axis, [(i, i ^ mask) for i in range(size)])

    def far_dp(j, value):
        pairs = []
        for source in range(dps):
            for member in range(tensors):
                target = source ^ (2 * (j + 1) + member % 2)
                pairs.append((source * tensors + member, target * tensors + member))
        return lax.ppermute(value, ("dp", "tensor"), pairs)

    far = dps // 2 - 1
    first = width * 14 // 16
    block = ranks // dps
    column_block = kv_width // (dps * tensors)
    group = max(column_block, lanes)
    extra = trials * dps * group + trials // 2 * ranks
    payload_shapes = [
        shape((2, select, width + (extra if a == 0 else 0)), bf16) for a in range(trials) for b in range(ys)
    ]
    gain = input_norm_weight[None, :]
    pick_operands = (
        trial_row_index,
        residual_rows,
        gain,
        keyvalue_gradient,
        adapter_up_weight,
        adapter_down_weight,
    )
    picked = pl.pallas_call(
        functools.partial(pick_kernel, trials, ys, dps, select, width, column_block),
        out_shape=payload_shapes + [shape((1, width // 2, ranks), bf16)] * 2,
        in_specs=in_hbm(6),
        out_specs=whole_vmem(len(payload_shapes) + 2),
        scratch_shapes=[pltpu.SMEM(trial_row_index.shape, jnp.int32)]
        + [pltpu.VMEM(value.shape, value.dtype) for value in pick_operands[1:5]]
        + [pltpu.SemaphoreType.DMA((7,))],
        compiler_params=params(32),
        name="pick",
    )(*[pltpu.with_memory_space_constraint(value, pltpu.HBM) for value in pick_operands])
    payloads, downs = picked[:-2], picked[-2:]
    mine = [payloads[0]] + [None] * (trials * ys - 1)
    for mask in range(1, trials * ys):
        a, b = mask // ys, mask % ys
        mine[mask] = over(("trial", "tensor"), trials * tensors, a * tensors + 2 * b, payloads[mask])
    other = [to_core(value) for value in mine]
    downs = [*downs, *[to_core(value) for value in downs]]

    pair, turned, *terms = pl.pallas_call(
        functools.partial(term_kernel, trials, ys, dps, select, width),
        out_shape=[shape((2, tokens, width), bf16), shape((ranks, tokens), bf16)]
        + [shape((2, block, first), bf16)] * far,
        in_specs=whole_vmem(2 * trials * ys),
        out_specs=whole_vmem(2 + far),
        scratch_shapes=[pltpu.VMEM((tokens, ranks), bf16), pltpu.VMEM((ranks, tokens), f32)],
        compiler_params=params(16),
        cost_estimate=cost(2 * 10**10, 2 * 10**7),
        name="terms",
    )(*mine, *other)
    down_far = [far_dp(j, terms[j]) for j in range(far)]
    rank_term = pl.pallas_call(
        rank_kernel,
        out_shape=shape((tokens, ranks), f32),
        in_specs=whole_vmem(5),
        out_specs=pl.BlockSpec(memory_space=pltpu.VMEM),
        compiler_params=params(4),
        cost_estimate=cost(0, 0),
        name="rank",
    )(pair, *downs)
    rank_sums = [rank_term] + [over("tensor", tensors, 2 * b, rank_term) for b in range(1, ys)]

    base_terms = pl.pallas_call(
        functools.partial(base_kernel, ys),
        out_shape=[shape((local, kv_width), f32)] * ys + [shape((local, kv_width), bf16)] * ys,
        in_specs=whole_vmem(2),
        out_specs=whole_vmem(2 * ys),
        scratch_shapes=[pltpu.VMEM((tokens, kv_width), f32)],
        compiler_params=params(8),
        cost_estimate=cost(0, 0),
        name="base",
    )(pair, keyvalue_weight)
    kept = base_terms[:ys]
    came = [None] * ys
    for b in [*range(1, ys), 0]:
        came[b] = to_core(base_terms[ys + b])
    base_sums = [kept[0], came[0]]
    for b in range(1, ys):
        paired = pl.pallas_call(
            pair_kernel,
            out_shape=shape((local, kv_width), bf16),
            in_specs=whole_vmem(2),
            out_specs=pl.BlockSpec(memory_space=pltpu.VMEM),
            compiler_params=params(4),
            cost_estimate=cost(0, 0),
            name="pair",
        )(kept[b], came[b])
        base_sums.append(over("tensor", tensors, 2 * b, paired))

    up_lanes = ranks // 2 // block * column_block
    down_own, up_own, near, *up_far = pl.pallas_call(
        functools.partial(up_kernel, trials, ys, dps, select, column_block),
        out_shape=[
            shape((block, width), f32),
            shape((ranks // 2, column_block), f32),
            shape((block, width + up_lanes), bf16),
        ]
        + [shape((2, block, width - first + up_lanes), bf16)] * far,
        in_specs=whole_vmem(3 * ys + 2),
        out_specs=whole_vmem(3 + far),
        scratch_shapes=[pltpu.VMEM((2, tokens, dps * group), bf16), pltpu.VMEM((2, ranks, dps * group), f32)],
        compiler_params=params(8),
        cost_estimate=cost(0, 0),
        name="up_terms",
    )(*rank_sums, *mine[:ys], *other[:ys], pair, turned)
    near = over("dp", dps, 1, near)
    up_far = [far_dp(j, up_far[j]) for j in range(far)]
    output = pl.pallas_call(
        functools.partial(output_kernel, ys),
        out_shape=shape((1, local, kv_width), f32),
        in_specs=whole_vmem(2 * ys + 2),
        out_specs=pl.BlockSpec(memory_space=pltpu.VMEM),
        compiler_params=params(8),
        cost_estimate=cost(0, 0),
        name="output",
    )(*rank_sums, *base_sums, adapter_up_weight)
    others = []
    for value, after in [(value, []) for value in down_far] + [(value, [near]) for value in up_far]:
        part = pl.pallas_call(
            split_kernel,
            out_shape=shape((block, max(value.shape[2], width // 2)), bf16),
            in_specs=whole_vmem(1 + len(after)),
            out_specs=pl.BlockSpec(memory_space=pltpu.VMEM),
            compiler_params=params(4),
            cost_estimate=cost(0, 0),
            name="split",
        )(value, *after)
        others.append(to_core(part))

    grad_a, grad_b = pl.pallas_call(
        functools.partial(sum_kernel, far),
        out_shape=[shape((1, block, width), f32), shape((1, ranks // 2, column_block), f32)],
        in_specs=whole_vmem(3 + 4 * far),
        out_specs=whole_vmem(2),
        compiler_params=params(8),
        cost_estimate=cost(0, 0),
        name="sums",
    )(down_own, up_own, near, *down_far, *up_far, *others)
    return output, grad_a, grad_b


def solution(mesh):
    return jax.shard_map(
        shards,
        mesh=mesh,
        in_specs=(
            P(("trial", "dp", "tensor"), None),
            P(),
            P(None, "dp"),
            P("tensor", None),
            P("trial", "tensor", None),
            P("trial", None, None),
            P("trial", ("dp", "tensor"), None),
        ),
        out_specs=(
            P("trial", ("dp", "tensor"), None),
            P("trial", "dp", "tensor"),
            P("trial", None, ("dp", "tensor")),
        ),
        check_vma=False,
    )
```

```python
import functools

import jax
import jax.numpy as jnp
from jax import lax
from jax.experimental import pallas as pl
from jax.experimental.pallas import tpu as pltpu
from jax.sharding import PartitionSpec as P

adapter_scale = 2.0
norm_eps = 1e-05
lanes = 128
f32 = jnp.float32
bf16 = jnp.bfloat16


def whole_vmem(count):
    return [pl.BlockSpec(memory_space=pltpu.VMEM)] * count


def params(mib):
    return pltpu.CompilerParams(vmem_limit_bytes=mib * 1024 * 1024)


def in_hbm(count):
    return [pl.BlockSpec(memory_space=pltpu.HBM)] * count


def cost(flops, moved):
    return pl.CostEstimate(flops=flops, bytes_accessed=moved, transcendentals=0)


def two_terms(value):
    high = value.astype(bf16)
    return high, (value - high.astype(f32)).astype(bf16)


def dot_rows(left, right):
    return lax.dot_general(left, right, (((0,), (0,)), ((), ())), preferred_element_type=f32)


def dot_last(left, right):
    return lax.dot_general(left, right, (((1,), (1,)), ((), ())), preferred_element_type=f32)


def pick_kernel(trials, ys, dps, select, width, column_block, index_hbm, rows_hbm, gain_hbm, grad_hbm, up_hbm, down_hbm, *rest):
    outs, rest = rest[:ys], rest[ys:]
    downs, normed_ref, hot_ref = rest[:2], *rest[2:4]
    index_ref, rows_ref, gain_ref, grad_ref, up_ref, sems = rest[4:]
    copies = [
        pltpu.make_async_copy(source, target, sems.at[i])
        for i, (source, target) in enumerate(
            (
                (index_hbm, index_ref),
                (rows_hbm, rows_ref),
                (gain_hbm, gain_ref),
                (grad_hbm, grad_ref),
                (up_hbm, up_ref),
                (down_hbm.at[:, : width // 2], downs[0]),
                (down_hbm.at[:, width // 2 :], downs[1]),
            )
        )
    ]
    for copy in copies:
        copy.start()
    trial, tensor = lax.axis_index("trial"), lax.axis_index("tensor")
    tensors = 2 * ys
    y = tensor // 2
    pool, features = rows_ref.shape
    start = (trial * tensors + tensor) * select
    column = lax.broadcasted_iota(jnp.int32, (select, pool), 1)
    row = lax.broadcasted_iota(jnp.int32, (select, pool), 0)
    hots = []
    copies[0].wait()
    for a in range(trials):
        picked = jnp.zeros((select, pool), jnp.int32)
        for i in range(select):
            picked = jnp.where(row == i, index_ref[trial ^ a, start + i], picked)
        hots.append(jnp.where(column == picked, 1.0, 0.0).astype(bf16))
    for n in range(1, trials):
        hot_ref[(n - 1) * select : n * select, :] = hots[n]
    square = jnp.zeros((pool, 1), f32)
    chunk = 1024
    copies[1].wait()
    for f in range(0, features, chunk):
        part = rows_ref[:, f : f + chunk].astype(f32)
        square += jnp.sum(part * part, axis=1, keepdims=True)
    scale = lax.rsqrt(square / features + norm_eps)
    half = grad_ref.shape[2] // 2
    rank = up_ref.shape[1]
    for copy in copies[2:5]:
        copy.wait()
    keys = adapter_scale * dot_last(grad_ref[0, :, :half], up_ref[0, :, :half])
    values = adapter_scale * dot_last(grad_ref[0, :, half:], up_ref[0, :, half:])
    for b in range(ys):
        for core in range(2):
            for f in range(0, width, chunk):
                at = pl.multiple_of((y ^ b) * (2 * width) + core * width + f, chunk)
                part = rows_ref[:, pl.ds(at, chunk)].astype(f32) * scale * gain_ref[:, pl.ds(at, chunk)]
                part = part.astype(bf16)
                normed_ref[:, pl.ds(at, chunk)] = part
                part = jnp.dot(hots[0], part, preferred_element_type=f32)
                outs[b][core, :, f : f + chunk] = part.astype(bf16)
    group = max(column_block, lanes)
    for b in range(ys):
        for j in range(trials // 2):
            for core in range(2):
                token = (2 * j + core) * select
                at = slice(token, token + select)
                for i in range(2):
                    for q in range(dps):
                        member = 2 * (y ^ b) + i
                        place = pl.multiple_of((q * tensors + member) * column_block // group * group, group)
                        lane = width + ((2 * j + i) * dps + q) * group
                        outs[b][core, :, lane : lane + group] = grad_ref[0, at, pl.ds(place, group)]
                lane = width + trials * dps * group + j * 2 * rank
                outs[b][core, :, lane : lane + rank] = keys[at].astype(bf16)
                outs[b][core, :, lane + rank : lane + 2 * rank] = values[at].astype(bf16)
    copies[5].wait()
    copies[6].wait()


def others_kernel(trials, ys, select, normed_ref, hot_ref, *outs):
    y = lax.axis_index("tensor") // 2
    width = outs[0].shape[2]
    chunk = 1024
    for b in range(ys):
        for core in range(2):
            for f in range(0, width, chunk):
                at = pl.multiple_of((y ^ b) * (2 * width) + core * width + f, chunk)
                part = jnp.dot(hot_ref[...], normed_ref[:, pl.ds(at, chunk)], preferred_element_type=f32)
                part = part.astype(bf16)
                for n in range(trials - 1):
                    outs[n * ys + b][core, :, f : f + chunk] = part[n * select : (n + 1) * select]


def term_kernel(trials, ys, dps, select, width, *refs):
    count = trials * ys
    far = dps // 2 - 1
    mine, other, refs = refs[:count], refs[count : 2 * count], refs[2 * count :]
    pair, turned_ref = refs[:2]
    terms = refs[2 : 2 + far]
    gradient, turned = refs[2 + far :]
    trial, dp, tensor = lax.axis_index("trial"), lax.axis_index("dp"), lax.axis_index("tensor")
    tensors = 2 * ys
    y, core = tensor // 2, tensor % 2
    ranks = gradient.shape[1]
    local = trials * select
    for a in range(trials):
        for b in range(ys):
            for refs_at, from_core in ((mine, core), (other, 1 - core)):
                ref = refs_at[a * ys + b]
                member = 2 * (y ^ b) + from_core
                at = pl.multiple_of(((trial ^ a) * tensors + member) * select, select)
                for i in range(2):
                    pair[i, pl.ds(at, select), :] = ref[i, :, :width]
                if a == 0:
                    for j in range(trials // 2):
                        lane = ref.shape[2] - (trials // 2 - j) * ranks
                        for i in range(2):
                            to = pl.multiple_of(member * local + (2 * j + i) * select, select)
                            gradient[pl.ds(to, select), :] = ref[i, :, lane : lane + ranks]
    block = ranks // dps
    turned[...] = gradient[...].astype(f32).T
    turned_ref[...] = turned[...].astype(bf16)
    for j in range(far):
        at = pl.multiple_of((dp ^ (2 * (j + 1) + core)) * block, block)
        part = turned[pl.ds(at, block), :].astype(bf16)
        for i in range(2):
            first = terms[j].shape[2]
            terms[j][i] = jnp.dot(part, pair[i, :, :first], preferred_element_type=f32).astype(bf16)


def rank_kernel(pair, *refs):
    downs, rank_ref = refs[:4], refs[4]
    core = lax.axis_index("tensor") % 2
    result = jnp.zeros(rank_ref.shape, f32)
    for n, ref in enumerate(downs):
        i = core if n < 2 else 1 - core
        size = ref.shape[1]
        result += jnp.dot(pair[i, :, n % 2 * size : (n % 2 + 1) * size], ref[0], preferred_element_type=f32)
    rank_ref[...] = result


def base_kernel(ys, pair, weight_ref, *refs):
    kept, sent, total = refs[:ys], refs[ys : 2 * ys], refs[-1]
    tensor = lax.axis_index("tensor")
    local, width = kept[0].shape
    chunk = 512
    for f in range(0, width, chunk):
        total[:, f : f + chunk] = jnp.dot(pair[tensor % 2], weight_ref[:, f : f + chunk], preferred_element_type=f32)
        for b in range(ys):
            for out, member in ((kept[b], tensor ^ (2 * b)), (sent[b], tensor ^ (2 * b + 1))):
                at = pl.multiple_of(member * local, local)
                out[:, f : f + chunk] = total[pl.ds(at, local), f : f + chunk].astype(out.dtype)


def pair_kernel(kept_ref, came_ref, out_ref):
    out_ref[...] = (kept_ref[...] + came_ref[...].astype(f32)).astype(bf16)


def up_kernel(trials, ys, dps, select, block, *refs):
    tensors = 2 * ys
    far = dps // 2 - 1
    rank_refs, mine, other = refs[:ys], refs[ys : 2 * ys], refs[2 * ys : 3 * ys]
    pair, turned_ref = refs[3 * ys : 3 * ys + 2]
    down_own, up_own, near = refs[3 * ys + 2 : 3 * ys + 5]
    outs, gradient, product = refs[3 * ys + 5 : -2], refs[-2], refs[-1]
    dp, tensor = lax.axis_index("dp"), lax.axis_index("tensor")
    y, core = tensor // 2, tensor % 2
    local = trials * select
    half = dps * tensors * block // 2
    width = pair.shape[2]
    ranks = rank_refs[0].shape[1]
    rank = ranks // 2
    down_block = ranks // dps
    group = max(block, lanes)
    ranks_sum = rank_refs[0][...]
    for ref in rank_refs[1:]:
        ranks_sum = ranks_sum + ref[...]
    high, low = two_terms(adapter_scale * ranks_sum.T)
    for i in range(2):
        for b in range(ys):
            for ref, from_core in ((mine[b], core), (other[b], 1 - core)):
                for j in range(trials // 2):
                    lane = width + (2 * j + i) * dps * group
                    for n in range(2):
                        token = (2 * (y ^ b) + from_core) * local + (2 * j + n) * select
                        at = pl.multiple_of(token, select)
                        gradient[i, pl.ds(at, select), :] = ref[n, :, lane : lane + dps * group]
    for i in range(2):
        values = gradient[i]
        product[i] = jnp.dot(high, values, preferred_element_type=f32) + jnp.dot(
            low, values, preferred_element_type=f32
        )

    def up_part(target, i):
        column = (target * tensors + 2 * y + i) * block
        upper = column // half
        at = pl.multiple_of(upper * rank, rank)
        part = product[i, pl.ds(at, rank), pl.ds(pl.multiple_of(target * group, group), group)]
        if group > block:
            inner = column % group
            result = part[:, :block]
            for n in range(1, group // block):
                result = jnp.where(inner == n * block, part[:, n * block : (n + 1) * block], result)
            part = result
        return part

    for j in range(far):
        size = outs[j].shape[2] - rank // down_block * block
        at = pl.multiple_of((dp ^ (2 * (j + 1) + core)) * down_block, down_block)
        for i in range(2):
            term = jnp.dot(turned_ref[pl.ds(at, down_block), :], pair[i, :, width - size :], preferred_element_type=f32)
            outs[j][i, :, :size] = term.astype(bf16)
            part = up_part(dp ^ (2 * (j + 1) + core), i).astype(bf16)
            for n in range(rank // down_block):
                lane = size + n * block
                outs[j][i, :, lane : lane + block] = part[n * down_block : (n + 1) * down_block]
    for target, out in ((dp ^ 1, near), (dp, None)):
        at = pl.multiple_of(target * down_block, down_block)
        term = jnp.dot(turned_ref[pl.ds(at, down_block), :], pair[core], preferred_element_type=f32)
        part = up_part(target, core)
        if out is None:
            down_own[...] = term
            up_own[...] = part
        else:
            out[:, :width] = term.astype(bf16)
            for n in range(rank // down_block):
                lane = width + n * block
                out[:, lane : lane + block] = part[n * down_block : (n + 1) * down_block].astype(bf16)


def output_kernel(ys, *refs):
    rank_refs, terms, up_ref, out_ref = refs[:ys], refs[ys:-2], refs[-2], refs[-1]
    tensor = lax.axis_index("tensor")
    local, width = terms[0].shape
    half = width // 2
    rank = up_ref.shape[1]
    at = pl.multiple_of(tensor * local, local)
    ranks = rank_refs[0][pl.ds(at, local), :]
    for ref in rank_refs[1:]:
        ranks = ranks + ref[pl.ds(at, local), :]
    high, low = two_terms(adapter_scale * ranks)
    chunk = 512
    for f in range(0, width, chunk):
        side = rank * (f // half)
        up = up_ref[0, :, f : f + chunk]
        result = terms[0][:, f : f + chunk]
        for ref in terms[1:]:
            result = result + ref[:, f : f + chunk].astype(f32)
        result = result + jnp.dot(high[:, side : side + rank], up, preferred_element_type=f32)
        result = result + jnp.dot(low[:, side : side + rank], up, preferred_element_type=f32)
        out_ref[0, :, f : f + chunk] = result


def split_kernel(*refs):
    term_ref, out_ref = refs[0], refs[-1]
    size = term_ref.shape[2]
    out_ref[:, :size] = term_ref[1 - lax.axis_index("tensor") % 2]
    if out_ref.shape[1] > size:
        out_ref[:, size:] = jnp.zeros((out_ref.shape[0], out_ref.shape[1] - size), bf16)


def sum_kernel(far, *refs):
    down_own, up_own, near = refs[:3]
    firsts, seconds = refs[3 : 3 + far], refs[3 + far : 3 + 2 * far]
    others, (down_out, up_out) = refs[3 + 2 * far : -2], refs[-2:]
    core = lax.axis_index("tensor") % 2
    down_block, width = down_own.shape
    rank, block = up_own.shape
    first = firsts[0].shape[2]

    def total(result, lane, size):
        result = result + near[:, lane : lane + size].astype(f32)
        for j in range(far):
            if lane < first:
                result = result + firsts[j][core].astype(f32) + others[j][...].astype(f32)
            else:
                at = slice(lane - first, lane - first + size)
                result = result + seconds[j][core, :, at].astype(f32) + others[far + j][:, at].astype(f32)
        return result

    down_out[0, :, :first] = total(down_own[:, :first], 0, first)
    down_out[0, :, first:] = total(down_own[:, first:], first, width - first)
    for n in range(rank // down_block):
        at = slice(n * down_block, (n + 1) * down_block)
        up_out[0, at, :] = total(up_own[at, :], width + n * block, block)


def shards(
    residual_rows,
    input_norm_weight,
    trial_row_index,
    keyvalue_weight,
    adapter_down_weight,
    adapter_up_weight,
    keyvalue_gradient,
):
    trials, dps, tensors = lax.axis_size("trial"), lax.axis_size("dp"), lax.axis_size("tensor")
    ys = tensors // 2
    pool, features = residual_rows.shape
    tokens = trial_row_index.shape[1]
    select = tokens // (trials * tensors)
    local = tokens // tensors
    width, kv_width = keyvalue_weight.shape
    ranks = adapter_down_weight.shape[2]
    shape = jax.ShapeDtypeStruct

    def to_core(value):
        return lax.ppermute(value, "tensor", [(i, i ^ 1) for i in range(tensors)])

    def over(axis, size, mask, value):
        return lax.ppermute(value, axis, [(i, i ^ mask) for i in range(size)])

    def far_dp(j, value):
        pairs = []
        for source in range(dps):
            for member in range(tensors):
                target = source ^ (2 * (j + 1) + member % 2)
                pairs.append((source * tensors + member, target * tensors + member))
        return lax.ppermute(value, ("dp", "tensor"), pairs)

    far = dps // 2 - 1
    first = width * 14 // 16
    block = ranks // dps
    column_block = kv_width // (dps * tensors)
    group = max(column_block, lanes)
    extra = trials * dps * group + trials // 2 * ranks
    payload_shapes = [
        shape((2, select, width + (extra if a == 0 else 0)), bf16) for a in range(trials) for b in range(ys)
    ]
    gain = input_norm_weight[None, :]
    pick_operands = (
        trial_row_index,
        residual_rows,
        gain,
        keyvalue_gradient,
        adapter_up_weight,
        adapter_down_weight,
    )
    picked = pl.pallas_call(
        functools.partial(pick_kernel, trials, ys, dps, select, width, column_block),
        out_shape=payload_shapes[:ys]
        + [shape((1, width // 2, ranks), bf16)] * 2
        + [shape((pool, features), bf16), shape(((trials - 1) * select, pool), bf16)],
        in_specs=in_hbm(6),
        out_specs=whole_vmem(ys + 4),
        scratch_shapes=[pltpu.SMEM(trial_row_index.shape, jnp.int32)]
        + [pltpu.VMEM(value.shape, value.dtype) for value in pick_operands[1:5]]
        + [pltpu.SemaphoreType.DMA((7,))],
        compiler_params=params(32),
        name="pick",
    )(*[pltpu.with_memory_space_constraint(value, pltpu.HBM) for value in pick_operands])
    downs = picked[ys : ys + 2]
    payloads = [
        *picked[:ys],
        *pl.pallas_call(
            functools.partial(others_kernel, trials, ys, select),
            out_shape=payload_shapes[ys:],
            in_specs=whole_vmem(2),
            out_specs=whole_vmem(len(payload_shapes) - ys),
            compiler_params=params(8),
            cost_estimate=cost(0, 0),
            name="pick_others",
        )(*picked[-2:]),
    ]
    mine = [payloads[0]] + [None] * (trials * ys - 1)
    for mask in range(1, trials * ys):
        a, b = mask // ys, mask % ys
        mine[mask] = over(("trial", "tensor"), trials * tensors, a * tensors + 2 * b, payloads[mask])
    other = [to_core(value) for value in mine]
    downs = [*downs, *[to_core(value) for value in downs]]

    pair, turned, *terms = pl.pallas_call(
        functools.partial(term_kernel, trials, ys, dps, select, width),
        out_shape=[shape((2, tokens, width), bf16), shape((ranks, tokens), bf16)]
        + [shape((2, block, first), bf16)] * far,
        in_specs=whole_vmem(2 * trials * ys),
        out_specs=whole_vmem(2 + far),
        scratch_shapes=[pltpu.VMEM((tokens, ranks), bf16), pltpu.VMEM((ranks, tokens), f32)],
        compiler_params=params(16),
        cost_estimate=cost(2 * 10**10, 2 * 10**7),
        name="terms",
    )(*mine, *other)
    down_far = [far_dp(j, terms[j]) for j in range(far)]
    rank_term = pl.pallas_call(
        rank_kernel,
        out_shape=shape((tokens, ranks), f32),
        in_specs=whole_vmem(5),
        out_specs=pl.BlockSpec(memory_space=pltpu.VMEM),
        compiler_params=params(4),
        cost_estimate=cost(0, 0),
        name="rank",
    )(pair, *downs)
    rank_sums = [rank_term] + [over("tensor", tensors, 2 * b, rank_term) for b in range(1, ys)]

    base_terms = pl.pallas_call(
        functools.partial(base_kernel, ys),
        out_shape=[shape((local, kv_width), f32)] * ys + [shape((local, kv_width), bf16)] * ys,
        in_specs=whole_vmem(2),
        out_specs=whole_vmem(2 * ys),
        scratch_shapes=[pltpu.VMEM((tokens, kv_width), f32)],
        compiler_params=params(8),
        cost_estimate=cost(0, 0),
        name="base",
    )(pair, keyvalue_weight)
    kept = base_terms[:ys]
    came = [None] * ys
    for b in [*range(1, ys), 0]:
        came[b] = to_core(base_terms[ys + b])
    base_sums = [kept[0], came[0]]
    for b in range(1, ys):
        paired = pl.pallas_call(
            pair_kernel,
            out_shape=shape((local, kv_width), bf16),
            in_specs=whole_vmem(2),
            out_specs=pl.BlockSpec(memory_space=pltpu.VMEM),
            compiler_params=params(4),
            cost_estimate=cost(0, 0),
            name="pair",
        )(kept[b], came[b])
        base_sums.append(over("tensor", tensors, 2 * b, paired))

    up_lanes = ranks // 2 // block * column_block
    down_own, up_own, near, *up_far = pl.pallas_call(
        functools.partial(up_kernel, trials, ys, dps, select, column_block),
        out_shape=[
            shape((block, width), f32),
            shape((ranks // 2, column_block), f32),
            shape((block, width + up_lanes), bf16),
        ]
        + [shape((2, block, width - first + up_lanes), bf16)] * far,
        in_specs=whole_vmem(3 * ys + 2),
        out_specs=whole_vmem(3 + far),
        scratch_shapes=[pltpu.VMEM((2, tokens, dps * group), bf16), pltpu.VMEM((2, ranks, dps * group), f32)],
        compiler_params=params(8),
        cost_estimate=cost(0, 0),
        name="up_terms",
    )(*rank_sums, *mine[:ys], *other[:ys], pair, turned)
    near = over("dp", dps, 1, near)
    up_far = [far_dp(j, up_far[j]) for j in range(far)]
    output = pl.pallas_call(
        functools.partial(output_kernel, ys),
        out_shape=shape((1, local, kv_width), f32),
        in_specs=whole_vmem(2 * ys + 2),
        out_specs=pl.BlockSpec(memory_space=pltpu.VMEM),
        compiler_params=params(8),
        cost_estimate=cost(0, 0),
        name="output",
    )(*rank_sums, *base_sums, adapter_up_weight)
    others = []
    for value, after in [(value, []) for value in down_far] + [(value, [near]) for value in up_far]:
        part = pl.pallas_call(
            split_kernel,
            out_shape=shape((block, max(value.shape[2], width // 2)), bf16),
            in_specs=whole_vmem(1 + len(after)),
            out_specs=pl.BlockSpec(memory_space=pltpu.VMEM),
            compiler_params=params(4),
            cost_estimate=cost(0, 0),
            name="split",
        )(value, *after)
        others.append(to_core(part))

    grad_a, grad_b = pl.pallas_call(
        functools.partial(sum_kernel, far),
        out_shape=[shape((1, block, width), f32), shape((1, ranks // 2, column_block), f32)],
        in_specs=whole_vmem(3 + 4 * far),
        out_specs=whole_vmem(2),
        compiler_params=params(8),
        cost_estimate=cost(0, 0),
        name="sums",
    )(down_own, up_own, near, *down_far, *up_far, *others)
    return output, grad_a, grad_b


def solution(mesh):
    return jax.shard_map(
        shards,
        mesh=mesh,
        in_specs=(
            P(("trial", "dp", "tensor"), None),
            P(),
            P(None, "dp"),
            P("tensor", None),
            P("trial", "tensor", None),
            P("trial", None, None),
            P("trial", ("dp", "tensor"), None),
        ),
        out_specs=(
            P("trial", ("dp", "tensor"), None),
            P("trial", "dp", "tensor"),
            P("trial", None, ("dp", "tensor")),
        ),
        check_vma=False,
    )
```

```python
import functools

import jax
import jax.numpy as jnp
from jax import lax
from jax.experimental import pallas as pl
from jax.experimental.pallas import tpu as pltpu
from jax.sharding import PartitionSpec as P

adapter_scale = 2.0
norm_eps = 1e-05
lanes = 128
f32 = jnp.float32
bf16 = jnp.bfloat16


def whole_vmem(count):
    return [pl.BlockSpec(memory_space=pltpu.VMEM)] * count


def params(mib):
    return pltpu.CompilerParams(vmem_limit_bytes=mib * 1024 * 1024)


def in_hbm(count):
    return [pl.BlockSpec(memory_space=pltpu.HBM)] * count


def cost(flops, moved):
    return pl.CostEstimate(flops=flops, bytes_accessed=moved, transcendentals=0)


def two_terms(value):
    high = value.astype(bf16)
    return high, (value - high.astype(f32)).astype(bf16)


def dot_rows(left, right):
    return lax.dot_general(left, right, (((0,), (0,)), ((), ())), preferred_element_type=f32)


def dot_last(left, right):
    return lax.dot_general(left, right, (((1,), (1,)), ((), ())), preferred_element_type=f32)


def pick_kernel(trials, ys, dps, select, width, column_block, index_hbm, rows_hbm, gain_hbm, grad_hbm, up_hbm, down_hbm, *rest):
    outs, rest = rest[:ys], rest[ys:]
    downs, normed_ref, hot_ref = rest[:2], *rest[2:4]
    index_ref, rows_ref, gain_ref, grad_ref, up_ref, sems = rest[4:]
    copies = [
        pltpu.make_async_copy(source, target, sems.at[i])
        for i, (source, target) in enumerate(
            (
                (index_hbm, index_ref),
                (rows_hbm, rows_ref),
                (gain_hbm, gain_ref),
                (grad_hbm, grad_ref),
                (up_hbm, up_ref),
                (down_hbm.at[:, : width // 2], downs[0]),
                (down_hbm.at[:, width // 2 :], downs[1]),
            )
        )
    ]
    for copy in copies:
        copy.start()
    trial, tensor = lax.axis_index("trial"), lax.axis_index("tensor")
    tensors = 2 * ys
    y = tensor // 2
    pool, features = rows_ref.shape
    start = (trial * tensors + tensor) * select
    column = lax.broadcasted_iota(jnp.int32, (select, pool), 1)
    row = lax.broadcasted_iota(jnp.int32, (select, pool), 0)
    hots = []
    copies[0].wait()
    for a in range(trials):
        picked = jnp.zeros((select, pool), jnp.int32)
        for i in range(select):
            picked = jnp.where(row == i, index_ref[trial ^ a, start + i], picked)
        hots.append(jnp.where(column == picked, 1.0, 0.0).astype(bf16))
    for n in range(1, trials):
        hot_ref[(n - 1) * select : n * select, :] = hots[n]
    square = jnp.zeros((pool, 1), f32)
    chunk = 1024
    copies[1].wait()
    for f in range(0, features, chunk):
        part = rows_ref[:, f : f + chunk].astype(f32)
        square += jnp.sum(part * part, axis=1, keepdims=True)
    scale = lax.rsqrt(square / features + norm_eps)
    half = grad_ref.shape[2] // 2
    rank = up_ref.shape[1]
    for copy in copies[2:5]:
        copy.wait()
    keys = adapter_scale * dot_last(grad_ref[0, :, :half], up_ref[0, :, :half])
    values = adapter_scale * dot_last(grad_ref[0, :, half:], up_ref[0, :, half:])
    for b in range(ys):
        for core in range(2):
            for f in range(0, width, chunk):
                at = pl.multiple_of((y ^ b) * (2 * width) + core * width + f, chunk)
                part = rows_ref[:, pl.ds(at, chunk)].astype(f32) * scale * gain_ref[:, pl.ds(at, chunk)]
                part = part.astype(bf16)
                normed_ref[:, pl.ds(at, chunk)] = part
                part = jnp.dot(hots[0], part, preferred_element_type=f32)
                outs[b][core, :, f : f + chunk] = part.astype(bf16)
    group = max(column_block, lanes)
    for b in range(ys):
        for j in range(trials // 2):
            for core in range(2):
                token = (2 * j + core) * select
                at = slice(token, token + select)
                for i in range(2):
                    for q in range(dps):
                        member = 2 * (y ^ b) + i
                        place = pl.multiple_of((q * tensors + member) * column_block // group * group, group)
                        lane = width + ((2 * j + i) * dps + q) * group
                        outs[b][core, :, lane : lane + group] = grad_ref[0, at, pl.ds(place, group)]
                lane = width + trials * dps * group + j * 2 * rank
                outs[b][core, :, lane : lane + rank] = keys[at].astype(bf16)
                outs[b][core, :, lane + rank : lane + 2 * rank] = values[at].astype(bf16)
    copies[5].wait()
    copies[6].wait()


def others_kernel(trials, ys, select, normed_ref, hot_ref, *outs):
    y = lax.axis_index("tensor") // 2
    width = outs[0].shape[2]
    chunk = 1024
    for b in range(ys):
        for core in range(2):
            for f in range(0, width, chunk):
                at = pl.multiple_of((y ^ b) * (2 * width) + core * width + f, chunk)
                part = jnp.dot(hot_ref[...], normed_ref[:, pl.ds(at, chunk)], preferred_element_type=f32)
                part = part.astype(bf16)
                for n in range(trials - 1):
                    outs[n * ys + b][core, :, f : f + chunk] = part[n * select : (n + 1) * select]


def term_kernel(trials, ys, dps, select, width, *refs):
    count = trials * ys
    far = dps // 2 - 1
    mine, other, refs = refs[:count], refs[count : 2 * count], refs[2 * count :]
    pair, turned_ref = refs[:2]
    terms = refs[2 : 2 + far]
    gradient, turned = refs[2 + far :]
    trial, dp, tensor = lax.axis_index("trial"), lax.axis_index("dp"), lax.axis_index("tensor")
    tensors = 2 * ys
    y, core = tensor // 2, tensor % 2
    ranks = gradient.shape[1]
    local = trials * select
    for a in range(trials):
        for b in range(ys):
            for refs_at, from_core in ((mine, core), (other, 1 - core)):
                ref = refs_at[a * ys + b]
                member = 2 * (y ^ b) + from_core
                at = pl.multiple_of(((trial ^ a) * tensors + member) * select, select)
                for i in range(2):
                    pair[i, pl.ds(at, select), :] = ref[i, :, :width]
                if a == 0:
                    for j in range(trials // 2):
                        lane = ref.shape[2] - (trials // 2 - j) * ranks
                        for i in range(2):
                            to = pl.multiple_of(member * local + (2 * j + i) * select, select)
                            gradient[pl.ds(to, select), :] = ref[i, :, lane : lane + ranks]
    block = ranks // dps
    turned[...] = gradient[...].astype(f32).T
    turned_ref[...] = turned[...].astype(bf16)
    for j in range(far):
        at = pl.multiple_of((dp ^ (2 * (j + 1) + core)) * block, block)
        part = turned[pl.ds(at, block), :].astype(bf16)
        for i in range(2):
            first = terms[j].shape[2]
            terms[j][i] = jnp.dot(part, pair[i, :, :first], preferred_element_type=f32).astype(bf16)


def rank_kernel(pair, *refs):
    downs, rank_ref = refs[:4], refs[4]
    core = lax.axis_index("tensor") % 2
    result = jnp.zeros(rank_ref.shape, f32)
    for n, ref in enumerate(downs):
        i = core if n < 2 else 1 - core
        size = ref.shape[1]
        result += jnp.dot(pair[i, :, n % 2 * size : (n % 2 + 1) * size], ref[0], preferred_element_type=f32)
    rank_ref[...] = result


def base_kernel(ys, pair, weight_ref, *refs):
    kept, sent, total = refs[:ys], refs[ys : 2 * ys], refs[-1]
    tensor = lax.axis_index("tensor")
    local, width = kept[0].shape
    chunk = 512
    for f in range(0, width, chunk):
        total[:, f : f + chunk] = jnp.dot(pair[tensor % 2], weight_ref[:, f : f + chunk], preferred_element_type=f32)
        for b in range(ys):
            for out, member in ((kept[b], tensor ^ (2 * b)), (sent[b], tensor ^ (2 * b + 1))):
                at = pl.multiple_of(member * local, local)
                out[:, f : f + chunk] = total[pl.ds(at, local), f : f + chunk].astype(out.dtype)


def pair_kernel(kept_ref, came_ref, out_ref):
    out_ref[...] = (kept_ref[...] + came_ref[...].astype(f32)).astype(bf16)


def up_kernel(trials, ys, dps, select, block, *refs):
    tensors = 2 * ys
    far = dps // 2 - 1
    rank_refs, mine, other = refs[:ys], refs[ys : 2 * ys], refs[2 * ys : 3 * ys]
    pair, turned_ref = refs[3 * ys : 3 * ys + 2]
    down_own, up_own, near = refs[3 * ys + 2 : 3 * ys + 5]
    outs, gradient, product = refs[3 * ys + 5 : -2], refs[-2], refs[-1]
    dp, tensor = lax.axis_index("dp"), lax.axis_index("tensor")
    y, core = tensor // 2, tensor % 2
    local = trials * select
    half = dps * tensors * block // 2
    width = pair.shape[2]
    ranks = rank_refs[0].shape[1]
    rank = ranks // 2
    down_block = ranks // dps
    group = max(block, lanes)
    ranks_sum = rank_refs[0][...]
    for ref in rank_refs[1:]:
        ranks_sum = ranks_sum + ref[...]
    high, low = two_terms(adapter_scale * ranks_sum.T)
    for i in range(2):
        for b in range(ys):
            for ref, from_core in ((mine[b], core), (other[b], 1 - core)):
                for j in range(trials // 2):
                    lane = width + (2 * j + i) * dps * group
                    for n in range(2):
                        token = (2 * (y ^ b) + from_core) * local + (2 * j + n) * select
                        at = pl.multiple_of(token, select)
                        gradient[i, pl.ds(at, select), :] = ref[n, :, lane : lane + dps * group]
    for i in range(2):
        values = gradient[i]
        product[i] = jnp.dot(high, values, preferred_element_type=f32) + jnp.dot(
            low, values, preferred_element_type=f32
        )

    def up_part(target, i):
        column = (target * tensors + 2 * y + i) * block
        upper = column // half
        at = pl.multiple_of(upper * rank, rank)
        part = product[i, pl.ds(at, rank), pl.ds(pl.multiple_of(target * group, group), group)]
        if group > block:
            inner = column % group
            result = part[:, :block]
            for n in range(1, group // block):
                result = jnp.where(inner == n * block, part[:, n * block : (n + 1) * block], result)
            part = result
        return part

    for j in range(far):
        size = outs[j].shape[2] - rank // down_block * block
        at = pl.multiple_of((dp ^ (2 * (j + 1) + core)) * down_block, down_block)
        for i in range(2):
            term = jnp.dot(turned_ref[pl.ds(at, down_block), :], pair[i, :, width - size :], preferred_element_type=f32)
            outs[j][i, :, :size] = term.astype(bf16)
            part = up_part(dp ^ (2 * (j + 1) + core), i).astype(bf16)
            for n in range(rank // down_block):
                lane = size + n * block
                outs[j][i, :, lane : lane + block] = part[n * down_block : (n + 1) * down_block]
    for target, out in ((dp ^ 1, near), (dp, None)):
        at = pl.multiple_of(target * down_block, down_block)
        term = jnp.dot(turned_ref[pl.ds(at, down_block), :], pair[core], preferred_element_type=f32)
        part = up_part(target, core)
        if out is None:
            down_own[...] = term
            up_own[...] = part
        else:
            out[:, :width] = term.astype(bf16)
            for n in range(rank // down_block):
                lane = width + n * block
                out[:, lane : lane + block] = part[n * down_block : (n + 1) * down_block].astype(bf16)


def output_kernel(ys, *refs):
    rank_refs, terms, up_ref, out_ref = refs[:ys], refs[ys:-2], refs[-2], refs[-1]
    tensor = lax.axis_index("tensor")
    local, width = terms[0].shape
    half = width // 2
    rank = up_ref.shape[1]
    at = pl.multiple_of(tensor * local, local)
    ranks = rank_refs[0][pl.ds(at, local), :]
    for ref in rank_refs[1:]:
        ranks = ranks + ref[pl.ds(at, local), :]
    terms_both = jnp.concatenate(two_terms(adapter_scale * ranks), axis=0)
    chunk = 512
    for f in range(0, width, chunk):
        side = rank * (f // half)
        up = up_ref[0, :, f : f + chunk]
        result = terms[0][:, f : f + chunk]
        for ref in terms[1:]:
            result = result + ref[:, f : f + chunk].astype(f32)
        both = jnp.dot(terms_both[:, side : side + rank], up, preferred_element_type=f32)
        out_ref[0, :, f : f + chunk] = result + both[:local] + both[local:]


def split_kernel(*refs):
    term_ref, out_ref = refs[0], refs[-1]
    size = term_ref.shape[2]
    out_ref[:, :size] = term_ref[1 - lax.axis_index("tensor") % 2]
    if out_ref.shape[1] > size:
        out_ref[:, size:] = jnp.zeros((out_ref.shape[0], out_ref.shape[1] - size), bf16)


def sum_kernel(far, *refs):
    down_own, up_own, near = refs[:3]
    firsts, seconds = refs[3 : 3 + far], refs[3 + far : 3 + 2 * far]
    others, (down_out, up_out) = refs[3 + 2 * far : -2], refs[-2:]
    core = lax.axis_index("tensor") % 2
    down_block, width = down_own.shape
    rank, block = up_own.shape
    first = firsts[0].shape[2]

    def total(result, lane, size):
        result = result + near[:, lane : lane + size].astype(f32)
        for j in range(far):
            if lane < first:
                result = result + firsts[j][core].astype(f32) + others[j][...].astype(f32)
            else:
                at = slice(lane - first, lane - first + size)
                result = result + seconds[j][core, :, at].astype(f32) + others[far + j][:, at].astype(f32)
        return result

    down_out[0, :, :first] = total(down_own[:, :first], 0, first)
    down_out[0, :, first:] = total(down_own[:, first:], first, width - first)
    for n in range(rank // down_block):
        at = slice(n * down_block, (n + 1) * down_block)
        up_out[0, at, :] = total(up_own[at, :], width + n * block, block)


def shards(
    residual_rows,
    input_norm_weight,
    trial_row_index,
    keyvalue_weight,
    adapter_down_weight,
    adapter_up_weight,
    keyvalue_gradient,
):
    trials, dps, tensors = lax.axis_size("trial"), lax.axis_size("dp"), lax.axis_size("tensor")
    ys = tensors // 2
    pool, features = residual_rows.shape
    tokens = trial_row_index.shape[1]
    select = tokens // (trials * tensors)
    local = tokens // tensors
    width, kv_width = keyvalue_weight.shape
    ranks = adapter_down_weight.shape[2]
    shape = jax.ShapeDtypeStruct

    def to_core(value):
        return lax.ppermute(value, "tensor", [(i, i ^ 1) for i in range(tensors)])

    def over(axis, size, mask, value):
        return lax.ppermute(value, axis, [(i, i ^ mask) for i in range(size)])

    def far_dp(j, value):
        pairs = []
        for source in range(dps):
            for member in range(tensors):
                target = source ^ (2 * (j + 1) + member % 2)
                pairs.append((source * tensors + member, target * tensors + member))
        return lax.ppermute(value, ("dp", "tensor"), pairs)

    far = dps // 2 - 1
    first = width * 14 // 16
    block = ranks // dps
    column_block = kv_width // (dps * tensors)
    group = max(column_block, lanes)
    extra = trials * dps * group + trials // 2 * ranks
    payload_shapes = [
        shape((2, select, width + (extra if a == 0 else 0)), bf16) for a in range(trials) for b in range(ys)
    ]
    gain = input_norm_weight[None, :]
    pick_operands = (
        trial_row_index,
        residual_rows,
        gain,
        keyvalue_gradient,
        adapter_up_weight,
        adapter_down_weight,
    )
    picked = pl.pallas_call(
        functools.partial(pick_kernel, trials, ys, dps, select, width, column_block),
        out_shape=payload_shapes[:ys]
        + [shape((1, width // 2, ranks), bf16)] * 2
        + [shape((pool, features), bf16), shape(((trials - 1) * select, pool), bf16)],
        in_specs=in_hbm(6),
        out_specs=whole_vmem(ys + 4),
        scratch_shapes=[pltpu.SMEM(trial_row_index.shape, jnp.int32)]
        + [pltpu.VMEM(value.shape, value.dtype) for value in pick_operands[1:5]]
        + [pltpu.SemaphoreType.DMA((7,))],
        compiler_params=params(32),
        name="pick",
    )(*[pltpu.with_memory_space_constraint(value, pltpu.HBM) for value in pick_operands])
    downs = picked[ys : ys + 2]
    payloads = [
        *picked[:ys],
        *pl.pallas_call(
            functools.partial(others_kernel, trials, ys, select),
            out_shape=payload_shapes[ys:],
            in_specs=whole_vmem(2),
            out_specs=whole_vmem(len(payload_shapes) - ys),
            compiler_params=params(8),
            cost_estimate=cost(0, 0),
            name="pick_others",
        )(*picked[-2:]),
    ]
    mine = [payloads[0]] + [None] * (trials * ys - 1)
    for mask in range(1, trials * ys):
        a, b = mask // ys, mask % ys
        mine[mask] = over(("trial", "tensor"), trials * tensors, a * tensors + 2 * b, payloads[mask])
    other = [to_core(value) for value in mine]
    downs = [*downs, *[to_core(value) for value in downs]]

    pair, turned, *terms = pl.pallas_call(
        functools.partial(term_kernel, trials, ys, dps, select, width),
        out_shape=[shape((2, tokens, width), bf16), shape((ranks, tokens), bf16)]
        + [shape((2, block, first), bf16)] * far,
        in_specs=whole_vmem(2 * trials * ys),
        out_specs=whole_vmem(2 + far),
        scratch_shapes=[pltpu.VMEM((tokens, ranks), bf16), pltpu.VMEM((ranks, tokens), f32)],
        compiler_params=params(16),
        cost_estimate=cost(2 * 10**10, 2 * 10**7),
        name="terms",
    )(*mine, *other)
    down_far = [far_dp(j, terms[j]) for j in range(far)]
    rank_term = pl.pallas_call(
        rank_kernel,
        out_shape=shape((tokens, ranks), f32),
        in_specs=whole_vmem(5),
        out_specs=pl.BlockSpec(memory_space=pltpu.VMEM),
        compiler_params=params(4),
        cost_estimate=cost(0, 0),
        name="rank",
    )(pair, *downs)
    rank_sums = [rank_term] + [over("tensor", tensors, 2 * b, rank_term) for b in range(1, ys)]

    base_terms = pl.pallas_call(
        functools.partial(base_kernel, ys),
        out_shape=[shape((local, kv_width), f32)] * ys + [shape((local, kv_width), bf16)] * ys,
        in_specs=whole_vmem(2),
        out_specs=whole_vmem(2 * ys),
        scratch_shapes=[pltpu.VMEM((tokens, kv_width), f32)],
        compiler_params=params(8),
        cost_estimate=cost(0, 0),
        name="base",
    )(pair, keyvalue_weight)
    kept = base_terms[:ys]
    came = [None] * ys
    for b in [*range(1, ys), 0]:
        came[b] = to_core(base_terms[ys + b])
    base_sums = [kept[0], came[0]]
    for b in range(1, ys):
        paired = pl.pallas_call(
            pair_kernel,
            out_shape=shape((local, kv_width), bf16),
            in_specs=whole_vmem(2),
            out_specs=pl.BlockSpec(memory_space=pltpu.VMEM),
            compiler_params=params(4),
            cost_estimate=cost(0, 0),
            name="pair",
        )(kept[b], came[b])
        base_sums.append(over("tensor", tensors, 2 * b, paired))

    up_lanes = ranks // 2 // block * column_block
    down_own, up_own, near, *up_far = pl.pallas_call(
        functools.partial(up_kernel, trials, ys, dps, select, column_block),
        out_shape=[
            shape((block, width), f32),
            shape((ranks // 2, column_block), f32),
            shape((block, width + up_lanes), bf16),
        ]
        + [shape((2, block, width - first + up_lanes), bf16)] * far,
        in_specs=whole_vmem(3 * ys + 2),
        out_specs=whole_vmem(3 + far),
        scratch_shapes=[pltpu.VMEM((2, tokens, dps * group), bf16), pltpu.VMEM((2, ranks, dps * group), f32)],
        compiler_params=params(8),
        cost_estimate=cost(0, 0),
        name="up_terms",
    )(*rank_sums, *mine[:ys], *other[:ys], pair, turned)
    near = over("dp", dps, 1, near)
    up_far = [far_dp(j, up_far[j]) for j in range(far)]
    output = pl.pallas_call(
        functools.partial(output_kernel, ys),
        out_shape=shape((1, local, kv_width), f32),
        in_specs=whole_vmem(2 * ys + 2),
        out_specs=pl.BlockSpec(memory_space=pltpu.VMEM),
        compiler_params=params(8),
        cost_estimate=cost(0, 0),
        name="output",
    )(*rank_sums, *base_sums, adapter_up_weight)
    others = []
    for value, after in [(value, []) for value in down_far] + [(value, [near]) for value in up_far]:
        part = pl.pallas_call(
            split_kernel,
            out_shape=shape((block, max(value.shape[2], width // 2)), bf16),
            in_specs=whole_vmem(1 + len(after)),
            out_specs=pl.BlockSpec(memory_space=pltpu.VMEM),
            compiler_params=params(4),
            cost_estimate=cost(0, 0),
            name="split",
        )(value, *after)
        others.append(to_core(part))

    grad_a, grad_b = pl.pallas_call(
        functools.partial(sum_kernel, far),
        out_shape=[shape((1, block, width), f32), shape((1, ranks // 2, column_block), f32)],
        in_specs=whole_vmem(3 + 4 * far),
        out_specs=whole_vmem(2),
        compiler_params=params(8),
        cost_estimate=cost(0, 0),
        name="sums",
    )(down_own, up_own, near, *down_far, *up_far, *others)
    return output, grad_a, grad_b


def solution(mesh):
    return jax.shard_map(
        shards,
        mesh=mesh,
        in_specs=(
            P(("trial", "dp", "tensor"), None),
            P(),
            P(None, "dp"),
            P("tensor", None),
            P("trial", "tensor", None),
            P("trial", None, None),
            P("trial", ("dp", "tensor"), None),
        ),
        out_specs=(
            P("trial", ("dp", "tensor"), None),
            P("trial", "dp", "tensor"),
            P("trial", None, ("dp", "tensor")),
        ),
        check_vma=False,
    )
```

```python
import functools

import jax
import jax.numpy as jnp
from jax import lax
from jax.experimental import pallas as pl
from jax.experimental.pallas import tpu as pltpu
from jax.sharding import PartitionSpec as P

adapter_scale = 2.0
norm_eps = 1e-05
lanes = 128
f32 = jnp.float32
bf16 = jnp.bfloat16


def whole_vmem(count):
    return [pl.BlockSpec(memory_space=pltpu.VMEM)] * count


def params(mib):
    return pltpu.CompilerParams(vmem_limit_bytes=mib * 1024 * 1024)


def in_hbm(count):
    return [pl.BlockSpec(memory_space=pltpu.HBM)] * count


def cost(flops, moved):
    return pl.CostEstimate(flops=flops, bytes_accessed=moved, transcendentals=0)


def two_terms(value):
    high = value.astype(bf16)
    return high, (value - high.astype(f32)).astype(bf16)


def dot_rows(left, right):
    return lax.dot_general(left, right, (((0,), (0,)), ((), ())), preferred_element_type=f32)


def dot_last(left, right):
    return lax.dot_general(left, right, (((1,), (1,)), ((), ())), preferred_element_type=f32)


def pick_kernel(trials, ys, dps, select, width, column_block, index_hbm, rows_hbm, gain_hbm, grad_hbm, up_hbm, down_hbm, *rest):
    outs, rest = rest[:ys], rest[ys:]
    downs, normed_ref, hot_ref = rest[:2], *rest[2:4]
    index_ref, rows_ref, gain_ref, grad_ref, up_ref, sems = rest[4:]
    copies = [
        pltpu.make_async_copy(source, target, sems.at[i])
        for i, (source, target) in enumerate(
            (
                (index_hbm, index_ref),
                (rows_hbm, rows_ref),
                (gain_hbm, gain_ref),
                (grad_hbm, grad_ref),
                (up_hbm, up_ref),
                (down_hbm.at[:, : width // 2], downs[0]),
                (down_hbm.at[:, width // 2 :], downs[1]),
            )
        )
    ]
    for copy in copies:
        copy.start()
    trial, tensor = lax.axis_index("trial"), lax.axis_index("tensor")
    tensors = 2 * ys
    y = tensor // 2
    pool, features = rows_ref.shape
    start = (trial * tensors + tensor) * select
    column = lax.broadcasted_iota(jnp.int32, (select, pool), 1)
    row = lax.broadcasted_iota(jnp.int32, (select, pool), 0)
    hots = []
    copies[0].wait()
    for a in range(trials):
        picked = jnp.zeros((select, pool), jnp.int32)
        for i in range(select):
            picked = jnp.where(row == i, index_ref[trial ^ a, start + i], picked)
        hots.append(jnp.where(column == picked, 1.0, 0.0).astype(bf16))
    for n in range(1, trials):
        hot_ref[(n - 1) * select : n * select, :] = hots[n]
    square = jnp.zeros((pool, 1), f32)
    chunk = 1024
    copies[1].wait()
    for f in range(0, features, chunk):
        part = rows_ref[:, f : f + chunk].astype(f32)
        square += jnp.sum(part * part, axis=1, keepdims=True)
    scale = lax.rsqrt(square / features + norm_eps)
    half = grad_ref.shape[2] // 2
    rank = up_ref.shape[1]
    for copy in copies[2:5]:
        copy.wait()
    keys = adapter_scale * dot_last(grad_ref[0, :, :half], up_ref[0, :, :half])
    values = adapter_scale * dot_last(grad_ref[0, :, half:], up_ref[0, :, half:])
    for b in range(ys):
        for core in range(2):
            for f in range(0, width, chunk):
                at = pl.multiple_of((y ^ b) * (2 * width) + core * width + f, chunk)
                part = rows_ref[:, pl.ds(at, chunk)].astype(f32) * scale * gain_ref[:, pl.ds(at, chunk)]
                part = part.astype(bf16)
                normed_ref[:, pl.ds(at, chunk)] = part
                part = jnp.dot(hots[0], part, preferred_element_type=f32)
                outs[b][core, :, f : f + chunk] = part.astype(bf16)
    group = max(column_block, lanes)
    for b in range(ys):
        for j in range(trials // 2):
            for core in range(2):
                token = (2 * j + core) * select
                at = slice(token, token + select)
                for i in range(2):
                    for q in range(dps):
                        member = 2 * (y ^ b) + i
                        place = pl.multiple_of((q * tensors + member) * column_block // group * group, group)
                        lane = width + ((2 * j + i) * dps + q) * group
                        outs[b][core, :, lane : lane + group] = grad_ref[0, at, pl.ds(place, group)]
                lane = width + trials * dps * group + j * 2 * rank
                outs[b][core, :, lane : lane + rank] = keys[at].astype(bf16)
                outs[b][core, :, lane + rank : lane + 2 * rank] = values[at].astype(bf16)
    copies[5].wait()
    copies[6].wait()


def others_kernel(trials, ys, select, normed_ref, hot_ref, *outs):
    y = lax.axis_index("tensor") // 2
    width = outs[0].shape[2]
    chunk = 1024
    for b in range(ys):
        for core in range(2):
            for f in range(0, width, chunk):
                at = pl.multiple_of((y ^ b) * (2 * width) + core * width + f, chunk)
                part = jnp.dot(hot_ref[...], normed_ref[:, pl.ds(at, chunk)], preferred_element_type=f32)
                part = part.astype(bf16)
                for n in range(trials - 1):
                    outs[n * ys + b][core, :, f : f + chunk] = part[n * select : (n + 1) * select]


def term_kernel(trials, ys, dps, select, width, *refs):
    count = trials * ys
    far = dps // 2 - 1
    mine, other, refs = refs[:count], refs[count : 2 * count], refs[2 * count :]
    pair, turned_ref = refs[:2]
    terms = refs[2 : 2 + far]
    gradient, turned = refs[2 + far :]
    trial, dp, tensor = lax.axis_index("trial"), lax.axis_index("dp"), lax.axis_index("tensor")
    tensors = 2 * ys
    y, core = tensor // 2, tensor % 2
    ranks = gradient.shape[1]
    local = trials * select
    for a in range(trials):
        for b in range(ys):
            for refs_at, from_core in ((mine, core), (other, 1 - core)):
                ref = refs_at[a * ys + b]
                member = 2 * (y ^ b) + from_core
                at = pl.multiple_of(((trial ^ a) * tensors + member) * select, select)
                for i in range(2):
                    pair[i, pl.ds(at, select), :] = ref[i, :, :width]
                if a == 0:
                    for j in range(trials // 2):
                        lane = ref.shape[2] - (trials // 2 - j) * ranks
                        for i in range(2):
                            to = pl.multiple_of(member * local + (2 * j + i) * select, select)
                            gradient[pl.ds(to, select), :] = ref[i, :, lane : lane + ranks]
    block = ranks // dps
    turned[...] = gradient[...].astype(f32).T
    turned_ref[...] = turned[...].astype(bf16)
    for j in range(far):
        at = pl.multiple_of((dp ^ (2 * (j + 1) + core)) * block, block)
        part = turned[pl.ds(at, block), :].astype(bf16)
        for i in range(2):
            first = terms[j].shape[2]
            terms[j][i] = jnp.dot(part, pair[i, :, :first], preferred_element_type=f32).astype(bf16)


def rank_kernel(pair, *refs):
    downs, rank_ref = refs[:4], refs[4]
    core = lax.axis_index("tensor") % 2
    result = jnp.zeros(rank_ref.shape, f32)
    for n, ref in enumerate(downs):
        i = core if n < 2 else 1 - core
        size = ref.shape[1]
        result += jnp.dot(pair[i, :, n % 2 * size : (n % 2 + 1) * size], ref[0], preferred_element_type=f32)
    rank_ref[...] = result


def base_kernel(ys, pair, weight_ref, *refs):
    kept, sent, total = refs[:ys], refs[ys : 2 * ys], refs[-1]
    tensor = lax.axis_index("tensor")
    local, width = kept[0].shape
    chunk = 512
    for f in range(0, width, chunk):
        total[:, f : f + chunk] = jnp.dot(pair[tensor % 2], weight_ref[:, f : f + chunk], preferred_element_type=f32)
        for b in range(ys):
            for out, member in ((kept[b], tensor ^ (2 * b)), (sent[b], tensor ^ (2 * b + 1))):
                at = pl.multiple_of(member * local, local)
                out[:, f : f + chunk] = total[pl.ds(at, local), f : f + chunk].astype(out.dtype)


def pair_kernel(kept_ref, came_ref, out_ref):
    out_ref[...] = (kept_ref[...] + came_ref[...].astype(f32)).astype(bf16)


def up_kernel(trials, ys, dps, select, block, *refs):
    tensors = 2 * ys
    far = dps // 2 - 1
    rank_refs, mine, other = refs[:ys], refs[ys : 2 * ys], refs[2 * ys : 3 * ys]
    pair, turned_ref = refs[3 * ys : 3 * ys + 2]
    down_own, up_own, near = refs[3 * ys + 2 : 3 * ys + 5]
    outs, gradient, product = refs[3 * ys + 5 : -2], refs[-2], refs[-1]
    dp, tensor = lax.axis_index("dp"), lax.axis_index("tensor")
    y, core = tensor // 2, tensor % 2
    local = trials * select
    half = dps * tensors * block // 2
    width = pair.shape[2]
    ranks = rank_refs[0].shape[1]
    rank = ranks // 2
    down_block = ranks // dps
    group = max(block, lanes)
    ranks_sum = rank_refs[0][...]
    for ref in rank_refs[1:]:
        ranks_sum = ranks_sum + ref[...]
    terms_both = jnp.concatenate(two_terms(adapter_scale * ranks_sum.T), axis=0)
    for i in range(2):
        for b in range(ys):
            for ref, from_core in ((mine[b], core), (other[b], 1 - core)):
                for j in range(trials // 2):
                    lane = width + (2 * j + i) * dps * group
                    for n in range(2):
                        token = (2 * (y ^ b) + from_core) * local + (2 * j + n) * select
                        at = pl.multiple_of(token, select)
                        gradient[i, pl.ds(at, select), :] = ref[n, :, lane : lane + dps * group]
    for i in range(2):
        values = gradient[i]
        both = jnp.dot(terms_both, values, preferred_element_type=f32)
        product[i] = both[:ranks] + both[ranks:]

    def up_part(target, i):
        column = (target * tensors + 2 * y + i) * block
        upper = column // half
        at = pl.multiple_of(upper * rank, rank)
        part = product[i, pl.ds(at, rank), pl.ds(pl.multiple_of(target * group, group), group)]
        if group > block:
            inner = column % group
            result = part[:, :block]
            for n in range(1, group // block):
                result = jnp.where(inner == n * block, part[:, n * block : (n + 1) * block], result)
            part = result
        return part

    for j in range(far):
        size = outs[j].shape[2] - rank // down_block * block
        at = pl.multiple_of((dp ^ (2 * (j + 1) + core)) * down_block, down_block)
        for i in range(2):
            term = jnp.dot(turned_ref[pl.ds(at, down_block), :], pair[i, :, width - size :], preferred_element_type=f32)
            outs[j][i, :, :size] = term.astype(bf16)
            part = up_part(dp ^ (2 * (j + 1) + core), i).astype(bf16)
            for n in range(rank // down_block):
                lane = size + n * block
                outs[j][i, :, lane : lane + block] = part[n * down_block : (n + 1) * down_block]
    for target, out in ((dp ^ 1, near), (dp, None)):
        at = pl.multiple_of(target * down_block, down_block)
        term = jnp.dot(turned_ref[pl.ds(at, down_block), :], pair[core], preferred_element_type=f32)
        part = up_part(target, core)
        if out is None:
            down_own[...] = term
            up_own[...] = part
        else:
            out[:, :width] = term.astype(bf16)
            for n in range(rank // down_block):
                lane = width + n * block
                out[:, lane : lane + block] = part[n * down_block : (n + 1) * down_block].astype(bf16)


def output_kernel(ys, *refs):
    rank_refs, terms, up_ref, out_ref = refs[:ys], refs[ys:-2], refs[-2], refs[-1]
    tensor = lax.axis_index("tensor")
    local, width = terms[0].shape
    half = width // 2
    rank = up_ref.shape[1]
    at = pl.multiple_of(tensor * local, local)
    ranks = rank_refs[0][pl.ds(at, local), :]
    for ref in rank_refs[1:]:
        ranks = ranks + ref[pl.ds(at, local), :]
    terms_both = jnp.concatenate(two_terms(adapter_scale * ranks), axis=0)
    chunk = 512
    for f in range(0, width, chunk):
        side = rank * (f // half)
        up = up_ref[0, :, f : f + chunk]
        result = terms[0][:, f : f + chunk]
        for ref in terms[1:]:
            result = result + ref[:, f : f + chunk].astype(f32)
        both = jnp.dot(terms_both[:, side : side + rank], up, preferred_element_type=f32)
        out_ref[0, :, f : f + chunk] = result + both[:local] + both[local:]


def split_kernel(*refs):
    term_ref, out_ref = refs[0], refs[-1]
    size = term_ref.shape[2]
    out_ref[:, :size] = term_ref[1 - lax.axis_index("tensor") % 2]
    if out_ref.shape[1] > size:
        out_ref[:, size:] = jnp.zeros((out_ref.shape[0], out_ref.shape[1] - size), bf16)


def sum_kernel(far, *refs):
    down_own, up_own, near = refs[:3]
    firsts, seconds = refs[3 : 3 + far], refs[3 + far : 3 + 2 * far]
    others, (down_out, up_out) = refs[3 + 2 * far : -2], refs[-2:]
    core = lax.axis_index("tensor") % 2
    down_block, width = down_own.shape
    rank, block = up_own.shape
    first = firsts[0].shape[2]

    def total(result, lane, size):
        result = result + near[:, lane : lane + size].astype(f32)
        for j in range(far):
            if lane < first:
                result = result + firsts[j][core].astype(f32) + others[j][...].astype(f32)
            else:
                at = slice(lane - first, lane - first + size)
                result = result + seconds[j][core, :, at].astype(f32) + others[far + j][:, at].astype(f32)
        return result

    down_out[0, :, :first] = total(down_own[:, :first], 0, first)
    down_out[0, :, first:] = total(down_own[:, first:], first, width - first)
    for n in range(rank // down_block):
        at = slice(n * down_block, (n + 1) * down_block)
        up_out[0, at, :] = total(up_own[at, :], width + n * block, block)


def shards(
    residual_rows,
    input_norm_weight,
    trial_row_index,
    keyvalue_weight,
    adapter_down_weight,
    adapter_up_weight,
    keyvalue_gradient,
):
    trials, dps, tensors = lax.axis_size("trial"), lax.axis_size("dp"), lax.axis_size("tensor")
    ys = tensors // 2
    pool, features = residual_rows.shape
    tokens = trial_row_index.shape[1]
    select = tokens // (trials * tensors)
    local = tokens // tensors
    width, kv_width = keyvalue_weight.shape
    ranks = adapter_down_weight.shape[2]
    shape = jax.ShapeDtypeStruct

    def to_core(value):
        return lax.ppermute(value, "tensor", [(i, i ^ 1) for i in range(tensors)])

    def over(axis, size, mask, value):
        return lax.ppermute(value, axis, [(i, i ^ mask) for i in range(size)])

    def far_dp(j, value):
        pairs = []
        for source in range(dps):
            for member in range(tensors):
                target = source ^ (2 * (j + 1) + member % 2)
                pairs.append((source * tensors + member, target * tensors + member))
        return lax.ppermute(value, ("dp", "tensor"), pairs)

    far = dps // 2 - 1
    first = width * 14 // 16
    block = ranks // dps
    column_block = kv_width // (dps * tensors)
    group = max(column_block, lanes)
    extra = trials * dps * group + trials // 2 * ranks
    payload_shapes = [
        shape((2, select, width + (extra if a == 0 else 0)), bf16) for a in range(trials) for b in range(ys)
    ]
    gain = input_norm_weight[None, :]
    pick_operands = (
        trial_row_index,
        residual_rows,
        gain,
        keyvalue_gradient,
        adapter_up_weight,
        adapter_down_weight,
    )
    picked = pl.pallas_call(
        functools.partial(pick_kernel, trials, ys, dps, select, width, column_block),
        out_shape=payload_shapes[:ys]
        + [shape((1, width // 2, ranks), bf16)] * 2
        + [shape((pool, features), bf16), shape(((trials - 1) * select, pool), bf16)],
        in_specs=in_hbm(6),
        out_specs=whole_vmem(ys + 4),
        scratch_shapes=[pltpu.SMEM(trial_row_index.shape, jnp.int32)]
        + [pltpu.VMEM(value.shape, value.dtype) for value in pick_operands[1:5]]
        + [pltpu.SemaphoreType.DMA((7,))],
        compiler_params=params(32),
        name="pick",
    )(*[pltpu.with_memory_space_constraint(value, pltpu.HBM) for value in pick_operands])
    downs = picked[ys : ys + 2]
    payloads = [
        *picked[:ys],
        *pl.pallas_call(
            functools.partial(others_kernel, trials, ys, select),
            out_shape=payload_shapes[ys:],
            in_specs=whole_vmem(2),
            out_specs=whole_vmem(len(payload_shapes) - ys),
            compiler_params=params(8),
            cost_estimate=cost(0, 0),
            name="pick_others",
        )(*picked[-2:]),
    ]
    mine = [payloads[0]] + [None] * (trials * ys - 1)
    for mask in range(1, trials * ys):
        a, b = mask // ys, mask % ys
        mine[mask] = over(("trial", "tensor"), trials * tensors, a * tensors + 2 * b, payloads[mask])
    other = [to_core(value) for value in mine]
    downs = [*downs, *[to_core(value) for value in downs]]

    pair, turned, *terms = pl.pallas_call(
        functools.partial(term_kernel, trials, ys, dps, select, width),
        out_shape=[shape((2, tokens, width), bf16), shape((ranks, tokens), bf16)]
        + [shape((2, block, first), bf16)] * far,
        in_specs=whole_vmem(2 * trials * ys),
        out_specs=whole_vmem(2 + far),
        scratch_shapes=[pltpu.VMEM((tokens, ranks), bf16), pltpu.VMEM((ranks, tokens), f32)],
        compiler_params=params(16),
        cost_estimate=cost(2 * 10**10, 2 * 10**7),
        name="terms",
    )(*mine, *other)
    down_far = [far_dp(j, terms[j]) for j in range(far)]
    rank_term = pl.pallas_call(
        rank_kernel,
        out_shape=shape((tokens, ranks), f32),
        in_specs=whole_vmem(5),
        out_specs=pl.BlockSpec(memory_space=pltpu.VMEM),
        compiler_params=params(4),
        cost_estimate=cost(0, 0),
        name="rank",
    )(pair, *downs)
    rank_sums = [rank_term] + [over("tensor", tensors, 2 * b, rank_term) for b in range(1, ys)]

    base_terms = pl.pallas_call(
        functools.partial(base_kernel, ys),
        out_shape=[shape((local, kv_width), f32)] * ys + [shape((local, kv_width), bf16)] * ys,
        in_specs=whole_vmem(2),
        out_specs=whole_vmem(2 * ys),
        scratch_shapes=[pltpu.VMEM((tokens, kv_width), f32)],
        compiler_params=params(8),
        cost_estimate=cost(0, 0),
        name="base",
    )(pair, keyvalue_weight)
    kept = base_terms[:ys]
    came = [None] * ys
    for b in [*range(1, ys), 0]:
        came[b] = to_core(base_terms[ys + b])
    base_sums = [kept[0], came[0]]
    for b in range(1, ys):
        paired = pl.pallas_call(
            pair_kernel,
            out_shape=shape((local, kv_width), bf16),
            in_specs=whole_vmem(2),
            out_specs=pl.BlockSpec(memory_space=pltpu.VMEM),
            compiler_params=params(4),
            cost_estimate=cost(0, 0),
            name="pair",
        )(kept[b], came[b])
        base_sums.append(over("tensor", tensors, 2 * b, paired))

    up_lanes = ranks // 2 // block * column_block
    down_own, up_own, near, *up_far = pl.pallas_call(
        functools.partial(up_kernel, trials, ys, dps, select, column_block),
        out_shape=[
            shape((block, width), f32),
            shape((ranks // 2, column_block), f32),
            shape((block, width + up_lanes), bf16),
        ]
        + [shape((2, block, width - first + up_lanes), bf16)] * far,
        in_specs=whole_vmem(3 * ys + 2),
        out_specs=whole_vmem(3 + far),
        scratch_shapes=[pltpu.VMEM((2, tokens, dps * group), bf16), pltpu.VMEM((2, ranks, dps * group), f32)],
        compiler_params=params(8),
        cost_estimate=cost(0, 0),
        name="up_terms",
    )(*rank_sums, *mine[:ys], *other[:ys], pair, turned)
    near = over("dp", dps, 1, near)
    up_far = [far_dp(j, up_far[j]) for j in range(far)]
    output = pl.pallas_call(
        functools.partial(output_kernel, ys),
        out_shape=shape((1, local, kv_width), f32),
        in_specs=whole_vmem(2 * ys + 2),
        out_specs=pl.BlockSpec(memory_space=pltpu.VMEM),
        compiler_params=params(8),
        cost_estimate=cost(0, 0),
        name="output",
    )(*rank_sums, *base_sums, adapter_up_weight)
    others = []
    for value, after in [(value, []) for value in down_far] + [(value, [near]) for value in up_far]:
        part = pl.pallas_call(
            split_kernel,
            out_shape=shape((block, max(value.shape[2], width // 2)), bf16),
            in_specs=whole_vmem(1 + len(after)),
            out_specs=pl.BlockSpec(memory_space=pltpu.VMEM),
            compiler_params=params(4),
            cost_estimate=cost(0, 0),
            name="split",
        )(value, *after)
        others.append(to_core(part))

    grad_a, grad_b = pl.pallas_call(
        functools.partial(sum_kernel, far),
        out_shape=[shape((1, block, width), f32), shape((1, ranks // 2, column_block), f32)],
        in_specs=whole_vmem(3 + 4 * far),
        out_specs=whole_vmem(2),
        compiler_params=params(8),
        cost_estimate=cost(0, 0),
        name="sums",
    )(down_own, up_own, near, *down_far, *up_far, *others)
    return output, grad_a, grad_b


def solution(mesh):
    return jax.shard_map(
        shards,
        mesh=mesh,
        in_specs=(
            P(("trial", "dp", "tensor"), None),
            P(),
            P(None, "dp"),
            P("tensor", None),
            P("trial", "tensor", None),
            P("trial", None, None),
            P("trial", ("dp", "tensor"), None),
        ),
        out_specs=(
            P("trial", ("dp", "tensor"), None),
            P("trial", "dp", "tensor"),
            P("trial", None, ("dp", "tensor")),
        ),
        check_vma=False,
    )
```
